256 devices in a mesh: pb: 64 (over y, x_hi, z), ka: 4 (over x_lo, core).
Axes of the slice: x: 4 (x_hi: 2, x_lo: 2; x = x_hi * 2 + x_lo), y: 4, z: 8, core: 2. Of those that a mesh axis runs over, the one named last changes fastest.
Arguments:
- queries: bfloat16 [32768, 256], P(('pb', 'ka')), may hold values from -6 to 6
- key_rows: bfloat16 [32768, 256], P(('pb', 'ka')), may hold values from -6 to 6
- value_rows: bfloat16 [32768, 256], P(('pb', 'ka')), may hold values from -6 to 6
- attn_output: bfloat16 [32768, 256], P(('pb', 'ka')), may hold values from -3 to 3
- grad_output: bfloat16 [32768, 256], P(('pb', 'ka')), as said below
- row_lse: float32 [2, 32768], P(None, ('pb', 'ka'))
Outputs:
- grad_query: bfloat16 [32768, 256], P(('pb', 'ka'))
- grad_keys: bfloat16 [32768, 256], P(('pb', 'ka'))
- grad_values: bfloat16 [32768, 256], P(('pb', 'ka'))
The draws below stay inside these ranges and needn't reach their ends.
Inputs may be any that keep to these rules, and one draw needn't show every extreme that they name: `grad_output`: loss-scaled output gradient, of order sqrt(32768) in magnitude.
All inputs are finite; a program needn't handle non-finite values.
Results may differ from the reference program's by a relative error of at most 0.0051.
Values may be sent and summed in bfloat16 or wider, within the bound.
No kernel may reach another device: no remote copies, remote signals or barrier semaphores. Data moves between devices by JAX's collectives and lax.ppermute only.
A program may use at most 64 MiB of HBM per device.

```python
import math
import jax
import jax.numpy as jnp
from jax import lax

DH = 128
HEADS = 2
SEQ = 32768
DM = 256


def draw_grad_output(key, part):
    key = jax.random.fold_in(key, 11)
    base_values = jnp.clip(jax.random.normal(key, (SEQ, DM), jnp.float32), -6.0, 6.0)
    return (base_values * (0.5 * math.sqrt(SEQ))).astype(jnp.bfloat16)


def draw_row_lse(key, part):
    key = jax.random.fold_in(key, 23)
    offsets = jax.random.uniform(key, (HEADS, SEQ), jnp.float32, -0.25, 0.25)
    return (math.log(SEQ) + 0.5 + offsets).astype(jnp.float32)


def block_scale(stream_key, extent, shards, low, high):
    loudness, own = 1.0, jax.random.fold_in(stream_key, 6)
    for position, shards_of in shards:
        heights = jnp.exp(jax.random.uniform(jax.random.fold_in(own, position), (shards_of,), jnp.float32, low / len(shards), high / len(shards)))
        loudness = loudness * jnp.repeat(heights, extent[position] // shards_of).reshape([-1 if axis == position else 1 for axis in range(len(extent))])
    return loudness


def gaussian(key, extent, width, limit, cuts=(), kind=jnp.bfloat16):
    drawn = width * jax.random.normal(key, extent, jnp.float32)
    if cuts:
        drawn = drawn * block_scale(key, extent, cuts, -0.22, 0.18)
    return jnp.clip(drawn, -limit, limit).astype(kind)


def setup_inputs(seed: int = 0) -> dict:
    splits = jax.random.split(jax.random.key(seed), 7)
    queries = gaussian(splits[0], (SEQ, DM), 1.0, 6.0, ((0, 256),))
    key_rows = gaussian(splits[1], (SEQ, DM), 1.0, 6.0, ((0, 256),))
    value_rows = gaussian(splits[2], (SEQ, DM), 1.0, 6.0, ((0, 256),))
    attn_output = gaussian(splits[3], (SEQ, DM), 0.5, 3.0, ((0, 256),))
    grad_output = draw_grad_output(jax.random.fold_in(splits[6], 71), 0)
    row_lse = draw_row_lse(jax.random.fold_in(splits[6], 71), 0)
    return dict(queries=queries, key_rows=key_rows, value_rows=value_rows, attn_output=attn_output, grad_output=grad_output, row_lse=row_lse)


def reference(queries, key_rows, value_rows, attn_output, grad_output, row_lse):
    seq_len = queries.shape[0]
    feature_width = queries.shape[1]
    score_scale = DH ** -0.5
    key_heads = key_rows.astype(jnp.float32).reshape(seq_len, HEADS, DH)
    value_heads = value_rows.astype(jnp.float32).reshape(seq_len, HEADS, DH)
    products = grad_output.astype(jnp.float32) * attn_output.astype(jnp.float32)
    row_delta = jnp.sum(products.reshape(seq_len, HEADS, DH), axis=2).T
    block_rows = math.gcd(seq_len, 512)
    block_total = seq_len // block_rows

    def advance(totals, block_index):
        grad_k, grad_v = totals
        offset = (block_index * block_rows).astype(jnp.int32)
        query_heads = lax.dynamic_slice_in_dim(queries, offset, block_rows, 0).astype(jnp.float32).reshape(block_rows, HEADS, DH)
        grad_heads = lax.dynamic_slice_in_dim(grad_output, offset, block_rows, 0).astype(jnp.float32).reshape(block_rows, HEADS, DH)
        lse_block = lax.dynamic_slice_in_dim(row_lse, offset, block_rows, 1)
        delta_block = lax.dynamic_slice_in_dim(row_delta, offset, block_rows, 1)
        scores = jnp.einsum("ihd,jhd->hij", query_heads, key_heads)
        attn_probs = jnp.exp(scores * score_scale - lse_block[:, :, None])
        probs_low = lax.optimization_barrier(attn_probs.astype(jnp.bfloat16)).astype(jnp.float32)
        grad_v = grad_v + jnp.einsum("hij,ihd->jhd", probs_low, grad_heads)
        dprobs = jnp.einsum("ihd,jhd->hij", grad_heads, value_heads)
        dscores = score_scale * attn_probs * (dprobs - delta_block[:, :, None])
        dscores_low = lax.optimization_barrier(dscores.astype(jnp.bfloat16)).astype(jnp.float32)
        grad_q = jnp.einsum("hij,jhd->ihd", dscores_low, key_heads)
        grad_k = grad_k + jnp.einsum("hij,ihd->jhd", dscores_low, query_heads)
        return (grad_k, grad_v), grad_q.reshape(block_rows, feature_width).astype(jnp.bfloat16)

    zeros_init = jnp.zeros((seq_len, HEADS, DH), jnp.float32)
    (grad_k, grad_v), grad_q_blocks = lax.scan(advance, (zeros_init, zeros_init), jnp.arange(block_total, dtype=jnp.int32))
    grad_query = grad_q_blocks.reshape(seq_len, feature_width)
    grad_keys = grad_k.reshape(seq_len, feature_width).astype(jnp.bfloat16)
    grad_values = grad_v.reshape(seq_len, feature_width).astype(jnp.bfloat16)
    return (grad_query, grad_keys, grad_values)
```

```python
import functools
import math

import jax
import jax.numpy as jnp
from jax import lax
from jax.experimental import pallas as pl
from jax.experimental.pallas import tpu as pltpu
from jax.sharding import Mesh, PartitionSpec as P

HEAD = 128
SCALE = HEAD**-0.5
LOG2E = math.log2(math.e)
AXES = ("y", "xh", "z", "xl", "core")
PLANE = ("y", "xh", "xl")
ROWS = 256
STATS = 16
NT = (((1,), (1,)), ((), ()))
F32, BF16 = jnp.float32, jnp.bfloat16


def split3(x):
    hi = lax.reduce_precision(x, 8, 7)
    mid = lax.reduce_precision(x - hi, 8, 7)
    low = x - hi - mid
    return [term.astype(BF16) for term in (hi, mid, low)]


def tile_kernel(first, last, chips, *refs):
    if first:
        qg_ref, kv1_ref, kv2_ref, dq_ref, d1_ref, d2_ref, acc_k, acc_v, kt_ref = refs
    else:
        qg_ref, kv1_ref, kv2_ref, old_ref, dq_ref, d1_ref, d2_ref, acc_k, acc_v, kt_ref = refs
    step = pl.program_id(0)
    k = jnp.concatenate([kv1_ref[:, :HEAD], kv2_ref[:, :HEAD]], axis=0)
    v = jnp.concatenate([kv1_ref[:, HEAD:], kv2_ref[:, HEAD:]], axis=0)

    @pl.when(step == 0)
    def _():
        acc_k[...] = jnp.zeros_like(acc_k)
        acc_v[...] = jnp.zeros_like(acc_v)
        kt_ref[...] = k.astype(F32).T.astype(BF16)

    kt = kt_ref[...]
    dk = acc_k[...]
    dv = acc_v[...]
    for chip in range(chips):
        q = qg_ref[chip, :ROWS, :HEAD]
        g = qg_ref[chip, :ROWS, HEAD:]
        stats = qg_ref[chip, ROWS:, :].astype(F32)
        lse = stats[0:1] + stats[1:2] + stats[2:3]
        delta = stats[3:4] + stats[4:5] + stats[5:6]
        s = lax.dot_general(k, q, NT, preferred_element_type=F32)
        p = jnp.exp2(s * (SCALE * LOG2E) - lse)
        dp = lax.dot_general(v, g, NT, preferred_element_type=F32)
        ds = (SCALE * p * (dp - delta)).astype(BF16)
        dv = dv + jnp.dot(p.astype(BF16), g, preferred_element_type=F32)
        dk = dk + jnp.dot(ds, q, preferred_element_type=F32)
        dq = jnp.dot(kt, ds, preferred_element_type=F32)
        if not first:
            dq = dq + old_ref[chip]
        dq_ref[chip] = dq.astype(dq_ref.dtype)
    acc_k[...] = dk
    acc_v[...] = dv

    @pl.when(step == pl.num_programs(0) - 1)
    def _():
        d1_ref[:, :HEAD] = dk[:ROWS].astype(BF16)
        d1_ref[:, HEAD:] = dv[:ROWS].astype(BF16)
        d2_ref[:, :HEAD] = dk[ROWS:].astype(BF16)
        d2_ref[:, HEAD:] = dv[ROWS:].astype(BF16)


def tile_call(qg, kv1, kv2, old, last):
    first = old is None
    groups, rows, width = qg.shape
    chips = 4
    q_spec = pl.BlockSpec((chips, rows, width), lambda i: (i, 0, 0))
    kv_spec = pl.BlockSpec((ROWS, width), lambda i: (0, 0))
    dq_spec = pl.BlockSpec((chips, HEAD, ROWS), lambda i: (i, 0, 0))
    pairs = groups * ROWS * 2 * ROWS
    return pl.pallas_call(
        functools.partial(tile_kernel, first, last, chips),
        grid=(groups // chips,),
        in_specs=[q_spec, kv_spec, kv_spec] + ([] if first else [dq_spec]),
        out_specs=[dq_spec, kv_spec, kv_spec],
        out_shape=[
            jax.ShapeDtypeStruct((groups, HEAD, ROWS), BF16 if last else F32),
            jax.ShapeDtypeStruct((ROWS, width), BF16),
            jax.ShapeDtypeStruct((ROWS, width), BF16),
        ],
        scratch_shapes=[
            pltpu.VMEM((2 * ROWS, HEAD), F32),
            pltpu.VMEM((2 * ROWS, HEAD), F32),
            pltpu.VMEM((HEAD, 2 * ROWS), BF16),
        ],
        compiler_params=pltpu.CompilerParams(vmem_limit_bytes=40 * 2**20),
        cost_estimate=pl.CostEstimate(
            flops=pairs * HEAD * 10, bytes_accessed=8 * 2**20, transcendentals=pairs
        ),
        name="tile",
    )(*((qg, kv1, kv2) if first else (qg, kv1, kv2, old)))


def shift(x, axis, by):
    n = lax.axis_size(axis)
    return lax.ppermute(x, axis, [(i, (i + by) % n) for i in range(n)])


def local(queries, key_rows, value_rows, attn_output, grad_output, row_lse):
    core = lax.axis_index("core")
    local_rows = queries.shape[0]
    products = grad_output.astype(F32) * attn_output.astype(F32)
    row_delta = jnp.sum(products.reshape(local_rows, 2, HEAD), axis=2).T
    stats = jnp.stack(split3(row_lse * LOG2E) + split3(row_delta), axis=1)
    stats = jnp.pad(stats, ((0, 0), (0, STATS - stats.shape[1]), (0, 0)))
    rows = jnp.concatenate([queries, grad_output, key_rows, value_rows], axis=0)
    even = core == 0
    heads = [
        jnp.concatenate([rows[:, h * HEAD : (h + 1) * HEAD], stats[h]], axis=0)
        for h in range(2)
    ]
    mine = jnp.where(even, heads[0], heads[1])
    other = shift(jnp.where(even, heads[1], heads[0]), "core", 1)

    def part(x, n):
        return x[n * local_rows : (n + 1) * local_rows]

    def pair(x, n):
        return jnp.concatenate([part(x, n), part(x, n + 1)], axis=1)

    query_pack = jnp.concatenate(
        [
            pair(mine, 0),
            pair(other, 0),
            jnp.concatenate([mine[4 * local_rows :], other[4 * local_rows :]], axis=1),
        ],
        axis=0,
    )
    key_pack = jnp.concatenate([pair(mine, 2), pair(other, 2)], axis=0)

    plane = math.prod(lax.axis_size(a) for a in PLANE)
    depth = lax.axis_size("z")
    spread = jnp.broadcast_to(query_pack[None], (plane,) + query_pack.shape)
    gathered = lax.all_to_all(spread, PLANE, 0, 0, tiled=True)
    keys = {0: key_pack}
    for by in (4, 3, 5, 2, 6, 1, 7):
        keys[by] = shift(key_pack, "z", by)

    total_q = None
    owned = []
    for a, b in ((4, 3), (5, 2), (6, 1), (7, 0)):
        total_q, da, db = tile_call(gathered, keys[a], keys[b], total_q, b == 0)
        for by, d in ((a, da), (b, db)):
            owned.append(shift(d, "z", depth - by) if by else d)
    returned = lax.all_to_all(total_q, PLANE, 0, 0, tiled=True)

    grad_kv = sum(d.astype(F32) for d in owned)
    grad_q = jnp.sum(returned.astype(F32), axis=0).T
    grads = jnp.stack([grad_q, grad_kv[:, :HEAD], grad_kv[:, HEAD:]]).astype(BF16)
    kept = grads[:, :local_rows]
    moved = shift(grads[:, local_rows:], "core", 1)
    out = jnp.concatenate(
        [jnp.where(even, kept, moved), jnp.where(even, moved, kept)], axis=2
    )
    return out[0], out[1], out[2]


def solution(mesh):
    devices = mesh.devices.reshape(4, 2, 8, 2, 2)
    torus = Mesh(devices, AXES)
    rows = P(AXES, None)
    return jax.shard_map(
        local,
        mesh=torus,
        in_specs=(rows, rows, rows, rows, rows, P(None, AXES)),
        out_specs=(rows, rows, rows),
        check_vma=False,
    )
```

```python
import functools
import math

import jax
import jax.numpy as jnp
from jax import lax
from jax.experimental import pallas as pl
from jax.experimental.pallas import tpu as pltpu
from jax.sharding import Mesh, PartitionSpec as P

HEAD = 128
SCALE = HEAD**-0.5
LOG2E = math.log2(math.e)
AXES = ("y", "xh", "z", "xl", "core")
PLANE = ("y", "xh", "xl")
ROWS = 256
STATS = 16
HALF = 128
NT = (((1,), (1,)), ((), ()))
F32, BF16 = jnp.float32, jnp.bfloat16


def split3(x):
    hi = x.astype(BF16)
    rest = x - hi.astype(F32)
    mid = rest.astype(BF16)
    low = (rest - mid.astype(F32)).astype(BF16)
    return jnp.concatenate([hi.astype(F32), mid.astype(F32), low.astype(F32)], axis=0)


def pack_kernel(core_ref, q_ref, k_ref, v_ref, o_ref, g_ref, lse_ref, qg_ref, kv_ref, send_ref):
    def fill(head, qg, kv):
        cols = slice(head * HEAD, (head + 1) * HEAD)
        g = g_ref[:, cols]
        products = g.astype(F32) * o_ref[:, cols].astype(F32)
        delta = jnp.sum(products.T, axis=0, keepdims=True)
        lse = lse_ref[head : head + 1, :] * LOG2E
        terms = jnp.concatenate([split3(lse), split3(delta)], axis=1)
        terms = jnp.concatenate([terms, jnp.zeros((STATS - 3, 2 * HALF), F32)], axis=0)
        qg[:HALF, :HEAD] = q_ref[:, cols]
        qg[:HALF, HEAD:] = g
        qg[HALF:, :] = terms.astype(BF16)
        kv[:, :HEAD] = k_ref[:, cols]
        kv[:, HEAD:] = v_ref[:, cols]

    send_qg = send_ref.at[: HALF + STATS]
    send_kv = send_ref.at[HALF + STATS :]
    for core in range(2):

        @pl.when(core_ref[0] == core)
        def _():
            fill(core, qg_ref, kv_ref)
            fill(1 - core, send_qg, send_kv)


def pack_call(core, *args):
    width = 2 * HEAD
    return pl.pallas_call(
        pack_kernel,
        in_specs=[pl.BlockSpec(memory_space=pltpu.SMEM)]
        + [pl.BlockSpec(memory_space=pltpu.VMEM)] * 6,
        out_specs=[pl.BlockSpec(memory_space=pltpu.VMEM)] * 3,
        out_shape=[
            jax.ShapeDtypeStruct((HALF + STATS, width), BF16),
            jax.ShapeDtypeStruct((HALF, width), BF16),
            jax.ShapeDtypeStruct((2 * HALF + STATS, width), BF16),
        ],
        name="pack",
    )(core.reshape(1), *args)


def tile_kernel(first, chips, *refs):
    if first:
        qg_ref, kv1_ref, kv2_ref, dq_ref, d1_ref, d2_ref, acc_k, acc_v, kt_ref = refs
    else:
        qg_ref, kv1_ref, kv2_ref, old_ref, _, dq_ref, d1_ref, d2_ref, acc_k, acc_v, kt_ref = refs
    step = pl.program_id(0)
    k = jnp.concatenate([kv1_ref[:, :HEAD], kv2_ref[:, :HEAD]], axis=0)
    v = jnp.concatenate([kv1_ref[:, HEAD:], kv2_ref[:, HEAD:]], axis=0)

    @pl.when(step == 0)
    def _():
        acc_k[...] = jnp.zeros_like(acc_k)
        acc_v[...] = jnp.zeros_like(acc_v)
        kt_ref[...] = k.astype(F32).T.astype(BF16)

    kt = kt_ref[...]
    dk = acc_k[...]
    dv = acc_v[...]
    for chip in range(chips):
        qs, gs, lses, deltas = [], [], [], []
        for base in (0, HALF + STATS):
            qs.append(qg_ref[chip, base : base + HALF, :HEAD])
            gs.append(qg_ref[chip, base : base + HALF, HEAD:])
            stats = qg_ref[chip, base + HALF : base + HALF + STATS, :].astype(F32)
            stats = stats[0:1] + stats[1:2] + stats[2:3]
            lses.append(stats[:, :HALF])
            deltas.append(stats[:, HALF:])
        q = jnp.concatenate(qs, axis=0)
        g = jnp.concatenate(gs, axis=0)
        lse = jnp.concatenate(lses, axis=1)
        delta = jnp.concatenate(deltas, axis=1)
        s = lax.dot_general(k, q, NT, preferred_element_type=F32)
        p = jnp.exp2(s * (SCALE * LOG2E) - lse)
        dp = lax.dot_general(v, g, NT, preferred_element_type=F32)
        ds = (SCALE * p * (dp - delta)).astype(BF16)
        dv = dv + jnp.dot(p.astype(BF16), g, preferred_element_type=F32)
        dk = dk + jnp.dot(ds, q, preferred_element_type=F32)
        dq = jnp.dot(kt, ds, preferred_element_type=F32)
        if not first:
            dq = dq + old_ref[chip]
        dq_ref[chip] = dq.astype(dq_ref.dtype)
    acc_k[...] = dk
    acc_v[...] = dv

    @pl.when(step == pl.num_programs(0) - 1)
    def _():
        d1_ref[:, :HEAD] = dk[:ROWS]
        d1_ref[:, HEAD:] = dv[:ROWS]
        d2_ref[:, :HEAD] = dk[ROWS:]
        d2_ref[:, HEAD:] = dv[ROWS:]


def tile_call(qg, kv1, kv2, old, after, last):
    first = old is None
    groups, rows, width = qg.shape
    chips = 4
    q_spec = pl.BlockSpec((chips, rows, width), lambda i: (i, 0, 0))
    kv_spec = pl.BlockSpec((ROWS, width), lambda i: (0, 0))
    dq_spec = pl.BlockSpec((chips, HEAD, ROWS), lambda i: (i, 0, 0))
    pairs = groups * ROWS * 2 * ROWS
    return pl.pallas_call(
        functools.partial(tile_kernel, first, chips),
        grid=(groups // chips,),
        in_specs=[q_spec, kv_spec, kv_spec]
        + ([] if first else [dq_spec, pl.BlockSpec(memory_space=pl.ANY)]),
        out_specs=[dq_spec, kv_spec, kv_spec],
        out_shape=[
            jax.ShapeDtypeStruct((groups, HEAD, ROWS), BF16 if last else F32),
            jax.ShapeDtypeStruct((ROWS, width), F32),
            jax.ShapeDtypeStruct((ROWS, width), F32),
        ],
        scratch_shapes=[
            pltpu.VMEM((2 * ROWS, HEAD), F32),
            pltpu.VMEM((2 * ROWS, HEAD), F32),
            pltpu.VMEM((HEAD, 2 * ROWS), BF16),
        ],
        compiler_params=pltpu.CompilerParams(vmem_limit_bytes=40 * 2**20),
        cost_estimate=pl.CostEstimate(
            flops=pairs * HEAD * 20, bytes_accessed=8 * 2**20, transcendentals=pairs
        ),
        name="tile",
    )(*((qg, kv1, kv2) if first else (qg, kv1, kv2, old, after)))


def shift(x, axis, by):
    n = lax.axis_size(axis)
    return lax.ppermute(x, axis, [(i, (i + by) % n) for i in range(n)])


def local(queries, key_rows, value_rows, attn_output, grad_output, row_lse):
    core = lax.axis_index("core")
    even = core == 0
    mine_q, mine_kv, send = pack_call(
        core, queries, key_rows, value_rows, attn_output, grad_output, row_lse
    )
    other = shift(send, "core", 1)
    query_pack = jnp.concatenate([mine_q, other[: HALF + STATS]], axis=0)
    key_pack = jnp.concatenate([mine_kv, other[HALF + STATS :]], axis=0)

    plane = math.prod(lax.axis_size(a) for a in PLANE)
    spread = jnp.broadcast_to(query_pack[None], (plane,) + query_pack.shape)
    gathered = lax.all_to_all(spread, PLANE, 0, 0, tiled=True)
    keys = {0: key_pack}
    for by in (1, 2, 3):
        keys[by] = shift(keys[by - 1], "z", 1)
        keys[-by] = shift(keys[1 - by], "z", -1)
    keys[4] = shift(keys[3], "z", 1)

    def low(x):
        return x.astype(BF16)

    total_q, far, own = tile_call(gathered, keys[4], keys[0], None, None, False)
    up = low(far)
    down = None
    after = up
    for by in (3, 2, 1):
        up_in = shift(up, "z", 1)
        down_in = None if down is None else shift(down, "z", -1)
        total_q, du, dd = tile_call(gathered, keys[-by], keys[by], total_q, after, by == 1)
        up = low(du + up_in.astype(F32))
        down = low(dd if down_in is None else dd + down_in.astype(F32))
        after = up
    returned = lax.all_to_all(total_q, PLANE, 0, 0, tiled=True)
    grad_kv = own + shift(up, "z", 1).astype(F32) + shift(down, "z", -1).astype(F32)

    grad_q = jnp.sum(returned.astype(F32), axis=0).T
    grads = jnp.stack([grad_q, grad_kv[:, :HEAD], grad_kv[:, HEAD:]]).astype(BF16)
    kept = grads[:, :HALF]
    moved = shift(grads[:, HALF:], "core", 1)
    out = jnp.concatenate(
        [jnp.where(even, kept, moved), jnp.where(even, moved, kept)], axis=2
    )
    return out[0], out[1], out[2]


def solution(mesh):
    devices = mesh.devices.reshape(4, 2, 8, 2, 2)
    torus = Mesh(devices, AXES)
    rows = P(AXES, None)
    return jax.shard_map(
        local,
        mesh=torus,
        in_specs=(rows, rows, rows, rows, rows, P(None, AXES)),
        out_specs=(rows, rows, rows),
        check_vma=False,
    )
```

```python
import functools
import math

import jax
import jax.numpy as jnp
from jax import lax
from jax.experimental import pallas as pl
from jax.experimental.pallas import tpu as pltpu
from jax.sharding import Mesh, PartitionSpec as P

HEAD = 128
SCALE = HEAD**-0.5
LOG2E = math.log2(math.e)
AXES = ("y", "xh", "z", "xl", "core")
GROUP = ("y", "xl")
ROWS = 256
STATS = 16
HALF = 128
NT = (((1,), (1,)), ((), ()))
F32, BF16 = jnp.float32, jnp.bfloat16


def split3(x):
    hi = x.astype(BF16)
    rest = x - hi.astype(F32)
    mid = rest.astype(BF16)
    low = (rest - mid.astype(F32)).astype(BF16)
    return jnp.concatenate([hi.astype(F32), mid.astype(F32), low.astype(F32)], axis=0)


def pack_kernel(core_ref, q_ref, k_ref, v_ref, o_ref, g_ref, lse_ref, qg_ref, kv_ref, send_ref):
    def fill(head, qg, kv):
        cols = slice(head * HEAD, (head + 1) * HEAD)
        g = g_ref[:, cols]
        products = g.astype(F32) * o_ref[:, cols].astype(F32)
        delta = jnp.sum(products.T, axis=0, keepdims=True)
        lse = lse_ref[head : head + 1, :] * LOG2E
        terms = jnp.concatenate([split3(lse), split3(delta)], axis=1)
        terms = jnp.concatenate([terms, jnp.zeros((STATS - 3, 2 * HALF), F32)], axis=0)
        qg[:HALF, :HEAD] = q_ref[:, cols]
        qg[:HALF, HEAD:] = g
        qg[HALF:, :] = terms.astype(BF16)
        kv[:, :HEAD] = k_ref[:, cols]
        kv[:, HEAD:] = v_ref[:, cols]

    send_qg = send_ref.at[: HALF + STATS]
    send_kv = send_ref.at[HALF + STATS :]
    for core in range(2):

        @pl.when(core_ref[0] == core)
        def _():
            fill(core, qg_ref, kv_ref)
            fill(1 - core, send_qg, send_kv)


def pack_call(core, *args):
    width = 2 * HEAD
    return pl.pallas_call(
        pack_kernel,
        in_specs=[pl.BlockSpec(memory_space=pltpu.SMEM)]
        + [pl.BlockSpec(memory_space=pltpu.VMEM)] * 6,
        out_specs=[pl.BlockSpec(memory_space=pltpu.VMEM)] * 3,
        out_shape=[
            jax.ShapeDtypeStruct((HALF + STATS, width), BF16),
            jax.ShapeDtypeStruct((HALF, width), BF16),
            jax.ShapeDtypeStruct((2 * HALF + STATS, width), BF16),
        ],
        name="pack",
    )(core.reshape(1), *args)


def spread_kernel(mine_ref, kv_ref, other_ref, out_ref, keys_ref):
    rows = HALF + STATS
    for n in range(out_ref.shape[0]):
        out_ref[n, :rows, :] = mine_ref[...]
        out_ref[n, rows:, :] = other_ref[:rows, :]
    keys_ref[:HALF, :] = kv_ref[...]
    keys_ref[HALF:, :] = other_ref[rows:, :]


def spread_call(n, *args):
    return pl.pallas_call(
        spread_kernel,
        in_specs=[pl.BlockSpec(memory_space=pltpu.VMEM)] * 3,
        out_specs=[pl.BlockSpec(memory_space=pltpu.VMEM)] * 2,
        out_shape=[
            jax.ShapeDtypeStruct((n, 2 * (HALF + STATS), 2 * HEAD), BF16),
            jax.ShapeDtypeStruct((ROWS, 2 * HEAD), BF16),
        ],
        name="spread",
    )(*args)


def tile_kernel(first, chips, *refs):
    if first:
        qg_ref, kv1_ref, kv2_ref, dq_ref, d1_ref, d2_ref, acc_k, acc_v, kt_ref = refs
    else:
        qg_ref, kv1_ref, kv2_ref, old_ref, _, dq_ref, d1_ref, d2_ref, acc_k, acc_v, kt_ref = refs
    step = pl.program_id(0)
    blocks = (kv1_ref, kv2_ref)

    @pl.when(step == 0)
    def _():
        acc_k[...] = jnp.zeros_like(acc_k)
        acc_v[...] = jnp.zeros_like(acc_v)
        for n, kv_ref in enumerate(blocks):
            kt_ref[n] = kv_ref[:, :HEAD].astype(F32).T.astype(BF16)

    for chip in range(chips):
        qs, gs, lses, deltas = [], [], [], []
        for base in (0, HALF + STATS):
            qs.append(qg_ref[chip, base : base + HALF, :HEAD])
            gs.append(qg_ref[chip, base : base + HALF, HEAD:])
            stats = qg_ref[chip, base + HALF : base + HALF + STATS, :].astype(F32)
            stats = stats[0:1] + stats[1:2] + stats[2:3]
            lses.append(stats[:, :HALF])
            deltas.append(stats[:, HALF:])
        q = jnp.concatenate(qs, axis=0)
        g = jnp.concatenate(gs, axis=0)
        lse = jnp.concatenate(lses, axis=1)
        delta = jnp.concatenate(deltas, axis=1)
        total = None if first else old_ref[chip]
        for n, kv_ref in enumerate(blocks):
            s = lax.dot_general(kv_ref[:, :HEAD], q, NT, preferred_element_type=F32)
            p = jnp.exp2(s * (SCALE * LOG2E) - lse)
            dp = lax.dot_general(kv_ref[:, HEAD:], g, NT, preferred_element_type=F32)
            ds = (SCALE * p * (dp - delta)).astype(BF16)
            acc_v[n] += jnp.dot(p.astype(BF16), g, preferred_element_type=F32)
            acc_k[n] += jnp.dot(ds, q, preferred_element_type=F32)
            dq = jnp.dot(kt_ref[n], ds, preferred_element_type=F32)
            total = dq if total is None else total + dq
        dq_ref[chip] = total.astype(dq_ref.dtype)

    @pl.when(step == pl.num_programs(0) - 1)
    def _():
        for n, d_ref in enumerate((d1_ref, d2_ref)):
            d_ref[:, :HEAD] = acc_k[n]
            d_ref[:, HEAD:] = acc_v[n]


def tile_call(qg, kv1, kv2, old, after, last):
    first = old is None
    groups, rows, width = qg.shape
    chips = 4
    q_spec = pl.BlockSpec((chips, rows, width), lambda i: (i, 0, 0))
    keys = kv1.shape[0]
    kv_spec = pl.BlockSpec((keys, width), lambda i: (0, 0))
    dq_spec = pl.BlockSpec((chips, HEAD, ROWS), lambda i: (i, 0, 0))
    pairs = groups * ROWS * 2 * keys
    return pl.pallas_call(
        functools.partial(tile_kernel, first, chips),
        grid=(groups // chips,),
        in_specs=[q_spec, kv_spec, kv_spec]
        + ([] if first else [dq_spec, pl.BlockSpec(memory_space=pl.ANY)]),
        out_specs=[dq_spec, kv_spec, kv_spec],
        out_shape=[
            jax.ShapeDtypeStruct((groups, HEAD, ROWS), BF16 if last else F32),
            jax.ShapeDtypeStruct((keys, width), F32),
            jax.ShapeDtypeStruct((keys, width), F32),
        ],
        scratch_shapes=[
            pltpu.VMEM((2, keys, HEAD), F32),
            pltpu.VMEM((2, keys, HEAD), F32),
            pltpu.VMEM((2, HEAD, keys), BF16),
        ],
        compiler_params=pltpu.CompilerParams(vmem_limit_bytes=40 * 2**20),
        cost_estimate=pl.CostEstimate(
            flops=pairs * HEAD * 20, bytes_accessed=8 * 2**20, transcendentals=pairs
        ),
        name="tile",
    )(*((qg, kv1, kv2) if first else (qg, kv1, kv2, old, after)))


def shift(x, axis, by):
    n = lax.axis_size(axis)
    return lax.ppermute(x, axis, [(i, (i + by) % n) for i in range(n)])


def local(queries, key_rows, value_rows, attn_output, grad_output, row_lse):
    core = lax.axis_index("core")
    even = core == 0
    mine_q, mine_kv, send = pack_call(
        core, queries, key_rows, value_rows, attn_output, grad_output, row_lse
    )
    other = shift(send, "core", 1)
    peers = math.prod(lax.axis_size(a) for a in GROUP)
    spread, key_pack = spread_call(peers, mine_q, mine_kv, other)
    key_pair = jnp.concatenate([key_pack, shift(key_pack, "xh", 1)], axis=0)
    gathered = lax.all_to_all(spread, GROUP, 0, 0, tiled=True)
    keys = {0: key_pair}
    for by in (1, 2, 3):
        keys[by] = shift(keys[by - 1], "z", 1)
        keys[-by] = shift(keys[1 - by], "z", -1)
    keys[4] = jnp.concatenate(
        [shift(keys[3][:ROWS], "z", 1), shift(keys[-3][ROWS:], "z", -1)], axis=0
    )

    def low(x):
        return x.astype(BF16)

    total_q, far, own = tile_call(gathered, keys[4], keys[0], None, None, False)
    up = low(far)
    down = None
    after = up
    for by in (3, 2, 1):
        up_in = shift(up, "z", 1)
        down_in = None if down is None else shift(down, "z", -1)
        total_q, du, dd = tile_call(gathered, keys[-by], keys[by], total_q, after, by == 1)
        up = low(du + up_in.astype(F32))
        down = low(dd if down_in is None else dd + down_in.astype(F32))
        after = up
    up_in = shift(up, "z", 1)
    down_in = shift(down, "z", -1)
    returned = lax.all_to_all(total_q, GROUP, 0, 0, tiled=True)
    grad_pair = own + up_in.astype(F32) + down_in.astype(F32)
    grad_kv = grad_pair[:ROWS] + shift(low(grad_pair[ROWS:]), "xh", 1).astype(F32)

    grad_q = jnp.sum(returned.astype(F32), axis=0).T
    grads = jnp.stack([grad_q, grad_kv[:, :HEAD], grad_kv[:, HEAD:]]).astype(BF16)
    kept = grads[:, :HALF]
    moved = shift(grads[:, HALF:], "core", 1)
    out = jnp.concatenate(
        [jnp.where(even, kept, moved), jnp.where(even, moved, kept)], axis=2
    )
    return out[0], out[1], out[2]


def solution(mesh):
    devices = mesh.devices.reshape(4, 2, 8, 2, 2)
    torus = Mesh(devices, AXES)
    rows = P(AXES, None)
    return jax.shard_map(
        local,
        mesh=torus,
        in_specs=(rows, rows, rows, rows, rows, P(None, AXES)),
        out_specs=(rows, rows, rows),
        check_vma=False,
    )
```

```python
import functools
import math

import jax
import jax.numpy as jnp
from jax import lax
from jax.experimental import pallas as pl
from jax.experimental.pallas import tpu as pltpu
from jax.sharding import Mesh, PartitionSpec as P

HEAD = 128
SCALE = HEAD**-0.5
LOG2E = math.log2(math.e)
AXES = ("y", "xh", "z", "xl", "core")
GROUP = ("y", "xl")
OWNERS = ("y", "xl", "core")
ROWS = 256
STATS = 16
HALF = 128
NT = (((1,), (1,)), ((), ()))
F32, BF16 = jnp.float32, jnp.bfloat16


def split3(x):
    hi = x.astype(BF16)
    rest = x - hi.astype(F32)
    mid = rest.astype(BF16)
    low = (rest - mid.astype(F32)).astype(BF16)
    return jnp.concatenate([hi.astype(F32), mid.astype(F32), low.astype(F32)], axis=0)


def pack_kernel(core_ref, q_ref, k_ref, v_ref, o_ref, g_ref, lse_ref, qg_ref, kv_ref, send_ref, far_ref):
    def fill(head, qg, kv):
        cols = slice(head * HEAD, (head + 1) * HEAD)
        g = g_ref[:, cols]
        products = g.astype(F32) * o_ref[:, cols].astype(F32)
        delta = jnp.sum(products.T, axis=0, keepdims=True)
        lse = lse_ref[head : head + 1, :] * LOG2E
        terms = jnp.concatenate([split3(lse), split3(delta)], axis=1)
        terms = jnp.concatenate([terms, jnp.zeros((STATS - 3, 2 * HALF), F32)], axis=0)
        qg[:HALF, :HEAD] = q_ref[:, cols]
        qg[:HALF, HEAD:] = g
        qg[HALF:, :] = terms.astype(BF16)
        kv[:, :HEAD] = k_ref[:, cols]
        kv[:, HEAD:] = v_ref[:, cols]

    send_qg = send_ref.at[: HALF + STATS]
    send_kv = send_ref.at[HALF + STATS :]
    for core in range(2):

        @pl.when(core_ref[0] == core)
        def _():
            fill(core, qg_ref, kv_ref)
            fill(1 - core, send_qg, send_kv)
            far_ref[...] = send_kv[...]


def pack_call(core, *args):
    width = 2 * HEAD
    return pl.pallas_call(
        pack_kernel,
        in_specs=[pl.BlockSpec(memory_space=pltpu.SMEM)]
        + [pl.BlockSpec(memory_space=pltpu.VMEM)] * 6,
        out_specs=[pl.BlockSpec(memory_space=pltpu.VMEM)] * 4,
        out_shape=[
            jax.ShapeDtypeStruct((HALF + STATS, width), BF16),
            jax.ShapeDtypeStruct((HALF, width), BF16),
            jax.ShapeDtypeStruct((2 * HALF + STATS, width), BF16),
            jax.ShapeDtypeStruct((HALF, width), BF16),
        ],
        name="pack",
    )(core.reshape(1), *args)


def spread_kernel(mine_ref, other_ref, out_ref):
    rows = HALF + STATS
    for n in range(out_ref.shape[0]):
        out_ref[n, :rows, :] = mine_ref[...]
        out_ref[n, rows:, :] = other_ref[:rows, :]


def spread_call(n, *args):
    return pl.pallas_call(
        spread_kernel,
        in_specs=[pl.BlockSpec(memory_space=pltpu.VMEM)] * 2,
        out_specs=pl.BlockSpec(memory_space=pltpu.VMEM),
        out_shape=jax.ShapeDtypeStruct((n, 2 * (HALF + STATS), 2 * HEAD), BF16),
        name="spread",
    )(*args)


def tile_kernel(count, first, last, chips, *refs):
    refs = list(refs)
    core_ref = refs.pop(0) if last else None
    qg_ref = refs.pop(0)
    blocks = [refs.pop(0) for _ in range(count)]
    if not first:
        old_ref = refs.pop(0)
        refs.pop(0)
    dq_ref = refs.pop(0)
    sums = [refs.pop(0) for _ in range(count)]
    acc_k, acc_v, kt_ref = refs
    step = pl.program_id(0)

    @pl.when(step == 0)
    def _():
        acc_k[...] = jnp.zeros_like(acc_k)
        acc_v[...] = jnp.zeros_like(acc_v)
        for n, kv_ref in enumerate(blocks):
            kt_ref[n] = kv_ref[:, :HEAD].astype(F32).T.astype(BF16)

    for chip in range(chips):
        qs, gs, lses, deltas = [], [], [], []
        for base in (0, HALF + STATS):
            qs.append(qg_ref[chip, base : base + HALF, :HEAD])
            gs.append(qg_ref[chip, base : base + HALF, HEAD:])
            stats = qg_ref[chip, base + HALF : base + HALF + STATS, :].astype(F32)
            stats = stats[0:1] + stats[1:2] + stats[2:3]
            lses.append(stats[:, :HALF])
            deltas.append(stats[:, HALF:])
        q = jnp.concatenate(qs, axis=0)
        g = jnp.concatenate(gs, axis=0)
        lse = jnp.concatenate(lses, axis=1)
        delta = jnp.concatenate(deltas, axis=1)
        total = None if first else old_ref[chip]
        for n, kv_ref in enumerate(blocks):
            s = lax.dot_general(kv_ref[:, :HEAD], q, NT, preferred_element_type=F32)
            p = jnp.exp2(s * (SCALE * LOG2E) - lse)
            dp = lax.dot_general(kv_ref[:, HEAD:], g, NT, preferred_element_type=F32)
            ds = (SCALE * p * (dp - delta)).astype(BF16)
            acc_v[n] += jnp.dot(p.astype(BF16), g, preferred_element_type=F32)
            acc_k[n] += jnp.dot(ds, q, preferred_element_type=F32)
            dq = jnp.dot(kt_ref[n], ds, preferred_element_type=F32)
            total = dq if total is None else total + dq
        if last:
            core = core_ref[0]
            dq_ref[2 * chip + core] = total[:, :HALF].astype(BF16)
            dq_ref[2 * chip + 1 - core] = total[:, HALF:].astype(BF16)
        else:
            dq_ref[chip] = total

    @pl.when(step == pl.num_programs(0) - 1)
    def _():
        for n, d_ref in enumerate(sums):
            d_ref[:, :HEAD] = acc_k[n]
            d_ref[:, HEAD:] = acc_v[n]


def tile_call(qg, blocks, old=None, after=None, core=None):
    first, last = old is None, core is not None
    groups, rows, width = qg.shape
    count, keys = len(blocks), blocks[0].shape[0]
    chips = 4
    q_spec = pl.BlockSpec((chips, rows, width), lambda i: (i, 0, 0))
    kv_spec = pl.BlockSpec((keys, width), lambda i: (0, 0))
    dq_spec = pl.BlockSpec((chips, HEAD, ROWS), lambda i: (i, 0, 0))
    dq_shape = jax.ShapeDtypeStruct((groups, HEAD, ROWS), F32)
    out_spec = dq_spec
    if last:
        out_spec = pl.BlockSpec((2 * chips, HEAD, HALF), lambda i: (i, 0, 0))
        dq_shape = jax.ShapeDtypeStruct((2 * groups, HEAD, HALF), BF16)
    args, specs = [qg, *blocks], [q_spec] + [kv_spec] * count
    if last:
        args, specs = [core.reshape(1)] + args, [pl.BlockSpec(memory_space=pltpu.SMEM)] + specs
    if not first:
        args += [old, after]
        specs += [dq_spec, pl.BlockSpec(memory_space=pl.ANY)]
    pairs = groups * ROWS * count * keys
    return pl.pallas_call(
        functools.partial(tile_kernel, count, first, last, chips),
        grid=(groups // chips,),
        in_specs=specs,
        out_specs=[out_spec] + [kv_spec] * count,
        out_shape=[dq_shape] + [jax.ShapeDtypeStruct((keys, width), F32)] * count,
        scratch_shapes=[
            pltpu.VMEM((count, keys, HEAD), F32),
            pltpu.VMEM((count, keys, HEAD), F32),
            pltpu.VMEM((count, HEAD, keys), BF16),
        ],
        compiler_params=pltpu.CompilerParams(vmem_limit_bytes=40 * 2**20),
        cost_estimate=pl.CostEstimate(
            flops=pairs * HEAD * 20, bytes_accessed=8 * 2**20, transcendentals=pairs
        ),
        name="tile",
    )(*args)


def shift(x, axis, by):
    n = lax.axis_size(axis)
    return lax.ppermute(x, axis, [(i, (i + by) % n) for i in range(n)])


def local(queries, key_rows, value_rows, attn_output, grad_output, row_lse):
    core = lax.axis_index("core")
    even = core == 0
    mine_q, mine_kv, send, far_kv = pack_call(
        core, queries, key_rows, value_rows, attn_output, grad_output, row_lse
    )
    corners = lax.axis_size("xh") * lax.axis_size("core")
    across = shift(mine_kv, "xh", 1)
    diagonal = lax.ppermute(
        far_kv, ("xh", "core"), [(i, corners - 1 - i) for i in range(corners)]
    )
    other = shift(send, "core", 1)
    key_pair = jnp.concatenate([mine_kv, other[HALF + STATS :], across, diagonal], axis=0)

    peers = math.prod(lax.axis_size(a) for a in GROUP)
    spread = spread_call(peers, mine_q, other)
    gathered = lax.all_to_all(spread, GROUP, 0, 0, tiled=True)
    keys = {0: key_pair}
    for by in (1, 2, 3):
        keys[by] = shift(keys[by - 1], "z", 1)
        keys[-by] = shift(keys[1 - by], "z", -1)
    keys[4] = jnp.concatenate(
        [shift(keys[3][:ROWS], "z", 1), shift(keys[-3][ROWS:], "z", -1)], axis=0
    )

    def low(x):
        return x.astype(BF16)

    total_q, own = tile_call(gathered, [keys[0]])
    total_q, far = tile_call(gathered, [keys[4]], total_q, keys[4])
    up = low(far)
    down = None
    after = up
    for by in (3, 2, 1):
        up_in = shift(up, "z", 1)
        down_in = None if down is None else shift(down, "z", -1)
        total_q, du, dd = tile_call(
            gathered, [keys[-by], keys[by]], total_q, after, core if by == 1 else None
        )
        up = low(du + up_in.astype(F32))
        down = low(dd if down_in is None else dd + down_in.astype(F32))
        after = up
    up_in = shift(up, "z", 1)
    down_in = shift(down, "z", -1)
    returned = lax.all_to_all(total_q, OWNERS, 0, 0, tiled=True)
    grad_pair = own + up_in.astype(F32) + down_in.astype(F32)
    grad_kv = grad_pair[:ROWS] + shift(low(grad_pair[ROWS:]), "xh", 1).astype(F32)
    grad_kv = low(grad_kv)
    kept = grad_kv[:HALF]
    moved = shift(grad_kv[HALF:], "core", 1)
    lower, upper = jnp.where(even, kept, moved), jnp.where(even, moved, kept)
    grad_k = jnp.concatenate([lower[:, :HEAD], upper[:, :HEAD]], axis=1)
    grad_v = jnp.concatenate([lower[:, HEAD:], upper[:, HEAD:]], axis=1)

    heads = returned.reshape(peers, 2 * HEAD, HALF).astype(F32)
    grad_q = low(jnp.sum(heads, axis=0).T)
    return grad_q, grad_k, grad_v


def solution(mesh):
    devices = mesh.devices.reshape(4, 2, 8, 2, 2)
    torus = Mesh(devices, AXES)
    rows = P(AXES, None)
    return jax.shard_map(
        local,
        mesh=torus,
        in_specs=(rows, rows, rows, rows, rows, P(None, AXES)),
        out_specs=(rows, rows, rows),
        check_vma=False,
    )
```

```python
import functools
import math

import jax
import jax.numpy as jnp
from jax import lax
from jax.experimental import pallas as pl
from jax.experimental.pallas import tpu as pltpu
from jax.sharding import Mesh, PartitionSpec as P

HEAD = 128
SCALE = HEAD**-0.5
LOG2E = math.log2(math.e)
AXES = ("y", "xh", "z", "xl", "core")
GROUP = ("y", "xl")
ROWS = 256
STATS = 16
HALF = 128
NT = (((1,), (1,)), ((), ()))
F32, BF16 = jnp.float32, jnp.bfloat16


def split3(x):
    hi = x.astype(BF16)
    rest = x - hi.astype(F32)
    mid = rest.astype(BF16)
    low = (rest - mid.astype(F32)).astype(BF16)
    return jnp.concatenate([hi.astype(F32), mid.astype(F32), low.astype(F32)], axis=0)


def pack_kernel(core_ref, q_ref, k_ref, v_ref, o_ref, g_ref, lse_ref, qg_ref, kv_ref, send_ref, far_ref):
    def fill(head, qg, kv):
        cols = slice(head * HEAD, (head + 1) * HEAD)
        g = g_ref[:, cols]
        products = g.astype(F32) * o_ref[:, cols].astype(F32)
        delta = jnp.sum(products.T, axis=0, keepdims=True)
        lse = lse_ref[head : head + 1, :] * LOG2E
        terms = jnp.concatenate([split3(lse), split3(delta)], axis=1)
        terms = jnp.concatenate([terms, jnp.zeros((STATS - 3, 2 * HALF), F32)], axis=0)
        qg[:HALF, :HEAD] = q_ref[:, cols]
        qg[:HALF, HEAD:] = g
        qg[HALF:, :] = terms.astype(BF16)
        kv[:, :HEAD] = k_ref[:, cols]
        kv[:, HEAD:] = v_ref[:, cols]

    send_qg = send_ref.at[: HALF + STATS]
    send_kv = send_ref.at[HALF + STATS :]
    for core in range(2):

        @pl.when(core_ref[0] == core)
        def _():
            fill(core, qg_ref, kv_ref)
            fill(1 - core, send_qg, send_kv)
            far_ref[...] = send_kv[...]


def pack_call(core, *args):
    width = 2 * HEAD
    return pl.pallas_call(
        pack_kernel,
        in_specs=[pl.BlockSpec(memory_space=pltpu.SMEM)]
        + [pl.BlockSpec(memory_space=pltpu.VMEM)] * 6,
        out_specs=[pl.BlockSpec(memory_space=pltpu.VMEM)] * 4,
        out_shape=[
            jax.ShapeDtypeStruct((HALF + STATS, width), BF16),
            jax.ShapeDtypeStruct((HALF, width), BF16),
            jax.ShapeDtypeStruct((2 * HALF + STATS, width), BF16),
            jax.ShapeDtypeStruct((HALF, width), BF16),
        ],
        name="pack",
    )(core.reshape(1), *args)


def spread_kernel(mine_ref, other_ref, out_ref):
    rows = HALF + STATS
    for n in range(out_ref.shape[0]):
        out_ref[n, :rows, :] = mine_ref[...]
        out_ref[n, rows:, :] = other_ref[:rows, :]


def spread_call(n, *args):
    return pl.pallas_call(
        spread_kernel,
        in_specs=[pl.BlockSpec(memory_space=pltpu.VMEM)] * 2,
        out_specs=pl.BlockSpec(memory_space=pltpu.VMEM),
        out_shape=jax.ShapeDtypeStruct((n, 2 * (HALF + STATS), 2 * HEAD), BF16),
        name="spread",
    )(*args)


def join_kernel(mine_ref, other_ref, across_ref, diagonal_ref, _, out_ref):
    out_ref[:HALF, :] = mine_ref[...]
    out_ref[HALF:ROWS, :] = other_ref[HALF + STATS :, :]
    out_ref[ROWS : ROWS + HALF, :] = across_ref[...]
    out_ref[ROWS + HALF :, :] = diagonal_ref[...]


def join_call(*args):
    vmem = pl.BlockSpec(memory_space=pltpu.VMEM)
    return pl.pallas_call(
        join_kernel,
        in_specs=[vmem] * 4 + [pl.BlockSpec(memory_space=pl.ANY)],
        out_specs=vmem,
        out_shape=jax.ShapeDtypeStruct((2 * ROWS, 2 * HEAD), BF16),
        name="join",
    )(*args)


def cut_kernel(low_ref, high_ref, _, first_ref, second_ref):
    first_ref[...] = low_ref[:ROWS, :]
    second_ref[...] = high_ref[ROWS:, :]


def cut_call(*args):
    vmem = pl.BlockSpec(memory_space=pltpu.VMEM)
    return pl.pallas_call(
        cut_kernel,
        in_specs=[vmem] * 2 + [pl.BlockSpec(memory_space=pl.ANY)],
        out_specs=[vmem] * 2,
        out_shape=[jax.ShapeDtypeStruct((ROWS, 2 * HEAD), BF16)] * 2,
        name="cut",
    )(*args)


def tile_kernel(count, first, chips, *refs):
    refs = list(refs)
    qg_ref = refs.pop(0)
    blocks = [refs.pop(0) for _ in range(count)]
    if not first:
        old_ref = refs.pop(0)
        refs.pop(0)
    dq_ref = refs.pop(0)
    sums = [refs.pop(0) for _ in range(count)]
    acc_k, acc_v, kt_ref = refs
    step = pl.program_id(0)

    @pl.when(step == 0)
    def _():
        acc_k[...] = jnp.zeros_like(acc_k)
        acc_v[...] = jnp.zeros_like(acc_v)
        for n, kv_ref in enumerate(blocks):
            kt_ref[n] = kv_ref[:, :HEAD].astype(F32).T.astype(BF16)

    for chip in range(chips):
        qs, gs, lses, deltas = [], [], [], []
        for base in (0, HALF + STATS):
            qs.append(qg_ref[chip, base : base + HALF, :HEAD])
            gs.append(qg_ref[chip, base : base + HALF, HEAD:])
            stats = qg_ref[chip, base + HALF : base + HALF + STATS, :].astype(F32)
            stats = stats[0:1] + stats[1:2] + stats[2:3]
            lses.append(stats[:, :HALF])
            deltas.append(stats[:, HALF:])
        q = jnp.concatenate(qs, axis=0)
        g = jnp.concatenate(gs, axis=0)
        lse = jnp.concatenate(lses, axis=1)
        delta = jnp.concatenate(deltas, axis=1)
        total = None if first else old_ref[chip]
        for n, kv_ref in enumerate(blocks):
            s = lax.dot_general(kv_ref[:, :HEAD], q, NT, preferred_element_type=F32)
            p = jnp.exp2(s * (SCALE * LOG2E) - lse)
            dp = lax.dot_general(kv_ref[:, HEAD:], g, NT, preferred_element_type=F32)
            ds = (SCALE * p * (dp - delta)).astype(BF16)
            acc_v[n] += jnp.dot(p.astype(BF16), g, preferred_element_type=F32)
            acc_k[n] += jnp.dot(ds, q, preferred_element_type=F32)
            dq = jnp.dot(kt_ref[n], ds, preferred_element_type=F32)
            total = dq if total is None else total + dq
        dq_ref[chip] = total.astype(dq_ref.dtype)

    @pl.when(step == pl.num_programs(0) - 1)
    def _():
        for n, d_ref in enumerate(sums):
            d_ref[:, :HEAD] = acc_k[n]
            d_ref[:, HEAD:] = acc_v[n]


def tile_call(qg, blocks, old=None, after=None, last=False):
    first = old is None
    groups, rows, width = qg.shape
    count, keys = len(blocks), blocks[0].shape[0]
    chips = 4
    q_spec = pl.BlockSpec((chips, rows, width), lambda i: (i, 0, 0))
    kv_spec = pl.BlockSpec((keys, width), lambda i: (0, 0))
    dq_spec = pl.BlockSpec((chips, HEAD, ROWS), lambda i: (i, 0, 0))
    dq_shape = jax.ShapeDtypeStruct((groups, HEAD, ROWS), BF16 if last else F32)
    args, specs = [qg, *blocks], [q_spec] + [kv_spec] * count
    if not first:
        args += [old, after]
        specs += [dq_spec, pl.BlockSpec(memory_space=pl.ANY)]
    pairs = groups * ROWS * count * keys
    return pl.pallas_call(
        functools.partial(tile_kernel, count, first, chips),
        grid=(groups // chips,),
        in_specs=specs,
        out_specs=[dq_spec] + [kv_spec] * count,
        out_shape=[dq_shape] + [jax.ShapeDtypeStruct((keys, width), F32)] * count,
        scratch_shapes=[
            pltpu.VMEM((count, keys, HEAD), F32),
            pltpu.VMEM((count, keys, HEAD), F32),
            pltpu.VMEM((count, HEAD, keys), BF16),
        ],
        compiler_params=pltpu.CompilerParams(vmem_limit_bytes=40 * 2**20),
        cost_estimate=pl.CostEstimate(
            flops=pairs * HEAD * 20, bytes_accessed=8 * 2**20, transcendentals=pairs
        ),
        name="tile",
    )(*args)


def shift(x, axis, by):
    n = lax.axis_size(axis)
    return lax.ppermute(x, axis, [(i, (i + by) % n) for i in range(n)])


def local(queries, key_rows, value_rows, attn_output, grad_output, row_lse):
    core = lax.axis_index("core")
    even = core == 0
    mine_q, mine_kv, send, far_kv = pack_call(
        core, queries, key_rows, value_rows, attn_output, grad_output, row_lse
    )
    corners = lax.axis_size("xh") * lax.axis_size("core")
    across = shift(mine_kv, "xh", 1)
    diagonal = lax.ppermute(
        far_kv, ("xh", "core"), [(i, corners - 1 - i) for i in range(corners)]
    )
    other = shift(send, "core", 1)
    peers = math.prod(lax.axis_size(a) for a in GROUP)
    spread = spread_call(peers, mine_q, other)
    gathered = lax.all_to_all(spread, GROUP, 0, 0, tiled=True)
    keys = {0: join_call(mine_kv, other, across, diagonal, spread)}
    for by in (1, 2, 3):
        keys[by] = shift(keys[by - 1], "z", 1)
        keys[-by] = shift(keys[1 - by], "z", -1)
    total_q, own = tile_call(gathered, [keys[0]])
    first_half, second_half = cut_call(keys[3], keys[-3], own)
    keys[4] = jnp.concatenate(
        [shift(first_half, "z", 1), shift(second_half, "z", -1)], axis=0
    )

    def low(x):
        return x.astype(BF16)

    total_q, far = tile_call(gathered, [keys[4]], total_q, keys[4])
    up = low(far)
    down = None
    after = up
    for by in (3, 2, 1):
        up_in = shift(up, "z", 1)
        down_in = None if down is None else shift(down, "z", -1)
        total_q, du, dd = tile_call(
            gathered, [keys[-by], keys[by]], total_q, after, by == 1
        )
        up = low(du + up_in.astype(F32))
        down = low(dd if down_in is None else dd + down_in.astype(F32))
        after = up
    up_in = shift(up, "z", 1)
    down_in = shift(down, "z", -1)
    returned = lax.all_to_all(total_q, GROUP, 0, 0, tiled=True)
    grad_pair = own + up_in.astype(F32) + down_in.astype(F32)
    grad_kv = grad_pair[:ROWS] + shift(low(grad_pair[ROWS:]), "xh", 1).astype(F32)

    grad_q = jnp.sum(returned.astype(F32), axis=0).T
    grads = jnp.stack([grad_q, grad_kv[:, :HEAD], grad_kv[:, HEAD:]]).astype(BF16)
    kept = grads[:, :HALF]
    moved = shift(grads[:, HALF:], "core", 1)
    out = jnp.concatenate(
        [jnp.where(even, kept, moved), jnp.where(even, moved, kept)], axis=2
    )
    return out[0], out[1], out[2]


def solution(mesh):
    devices = mesh.devices.reshape(4, 2, 8, 2, 2)
    torus = Mesh(devices, AXES)
    rows = P(AXES, None)
    return jax.shard_map(
        local,
        mesh=torus,
        in_specs=(rows, rows, rows, rows, rows, P(None, AXES)),
        out_specs=(rows, rows, rows),
        check_vma=False,
    )
```

```python
import functools
import math

import jax
import jax.numpy as jnp
from jax import lax
from jax.experimental import pallas as pl
from jax.experimental.pallas import tpu as pltpu
from jax.sharding import Mesh, PartitionSpec as P

HEAD = 128
SCALE = HEAD**-0.5
LOG2E = math.log2(math.e)
AXES = ("y", "xh", "z", "xl", "core")
GROUP = ("y", "xl")
ROWS = 256
STATS = 16
HALF = 128
NT = (((1,), (1,)), ((), ()))
F32, BF16 = jnp.float32, jnp.bfloat16


def split3(x):
    hi = x.astype(BF16)
    rest = x - hi.astype(F32)
    mid = rest.astype(BF16)
    low = (rest - mid.astype(F32)).astype(BF16)
    return jnp.concatenate([hi.astype(F32), mid.astype(F32), low.astype(F32)], axis=0)


def pack_kernel(core_ref, q_ref, k_ref, v_ref, o_ref, g_ref, lse_ref, qg_ref, kv_ref, send_ref, far_ref):
    def fill(head, qg, kv):
        cols = slice(head * HEAD, (head + 1) * HEAD)
        g = g_ref[:, cols]
        products = g.astype(F32) * o_ref[:, cols].astype(F32)
        delta = jnp.sum(products.T, axis=0, keepdims=True)
        lse = lse_ref[head : head + 1, :] * LOG2E
        terms = jnp.concatenate([split3(lse), split3(delta)], axis=1)
        terms = jnp.concatenate([terms, jnp.zeros((STATS - 3, 2 * HALF), F32)], axis=0)
        qg[:HALF, :HEAD] = q_ref[:, cols]
        qg[:HALF, HEAD:] = g
        qg[HALF:, :] = terms.astype(BF16)
        kv[:, :HEAD] = k_ref[:, cols]
        kv[:, HEAD:] = v_ref[:, cols]

    send_qg = send_ref.at[: HALF + STATS]
    send_kv = send_ref.at[HALF + STATS :]
    for core in range(2):

        @pl.when(core_ref[0] == core)
        def _():
            fill(core, qg_ref, kv_ref)
            fill(1 - core, send_qg, send_kv)
            far_ref[...] = send_kv[...]


def pack_call(core, *args):
    width = 2 * HEAD
    return pl.pallas_call(
        pack_kernel,
        in_specs=[pl.BlockSpec(memory_space=pltpu.SMEM)]
        + [pl.BlockSpec(memory_space=pltpu.VMEM)] * 6,
        out_specs=[pl.BlockSpec(memory_space=pltpu.VMEM)] * 4,
        out_shape=[
            jax.ShapeDtypeStruct((HALF + STATS, width), BF16),
            jax.ShapeDtypeStruct((HALF, width), BF16),
            jax.ShapeDtypeStruct((2 * HALF + STATS, width), BF16),
            jax.ShapeDtypeStruct((HALF, width), BF16),
        ],
        name="pack",
    )(core.reshape(1), *args)


def spread_kernel(mine_ref, other_ref, across_ref, diagonal_ref, out_ref, keys_ref):
    rows = HALF + STATS
    for n in range(out_ref.shape[0]):
        out_ref[n, :rows, :] = mine_ref[...]
        out_ref[n, rows:, :] = other_ref[:rows, :]
    keys_ref[:HALF, :] = across_ref[...]
    keys_ref[HALF:, :] = diagonal_ref[...]


def spread_call(n, *args):
    return pl.pallas_call(
        spread_kernel,
        in_specs=[pl.BlockSpec(memory_space=pltpu.VMEM)] * 4,
        out_specs=[pl.BlockSpec(memory_space=pltpu.VMEM)] * 2,
        out_shape=[
            jax.ShapeDtypeStruct((n, 2 * (HALF + STATS), 2 * HEAD), BF16),
            jax.ShapeDtypeStruct((ROWS, 2 * HEAD), BF16),
        ],
        name="spread",
    )(*args)


def tile_kernel(first, chips, *refs):
    refs = list(refs)
    qg_ref = refs.pop(0)
    blocks = [(refs.pop(0), refs.pop(0)) for _ in range(2)]
    if not first:
        old_ref = refs.pop(0)
        refs.pop(0)
    dq_ref, d1_ref, d2_ref, acc_k, acc_v, kt_ref = refs
    step = pl.program_id(0)

    def part(block, cols):
        return jnp.concatenate([ref[:, cols] for ref in block], axis=0)

    @pl.when(step == 0)
    def _():
        acc_k[...] = jnp.zeros_like(acc_k)
        acc_v[...] = jnp.zeros_like(acc_v)
        for n, block in enumerate(blocks):
            kt_ref[n] = part(block, slice(0, HEAD)).astype(F32).T.astype(BF16)

    for chip in range(chips):
        qs, gs, lses, deltas = [], [], [], []
        for base in (0, HALF + STATS):
            qs.append(qg_ref[chip, base : base + HALF, :HEAD])
            gs.append(qg_ref[chip, base : base + HALF, HEAD:])
            stats = qg_ref[chip, base + HALF : base + HALF + STATS, :].astype(F32)
            stats = stats[0:1] + stats[1:2] + stats[2:3]
            lses.append(stats[:, :HALF])
            deltas.append(stats[:, HALF:])
        q = jnp.concatenate(qs, axis=0)
        g = jnp.concatenate(gs, axis=0)
        lse = jnp.concatenate(lses, axis=1)
        delta = jnp.concatenate(deltas, axis=1)
        total = None if first else old_ref[chip]
        for n, block in enumerate(blocks):
            k, v = part(block, slice(0, HEAD)), part(block, slice(HEAD, 2 * HEAD))
            s = lax.dot_general(k, q, NT, preferred_element_type=F32)
            p = jnp.exp2(s * (SCALE * LOG2E) - lse)
            dp = lax.dot_general(v, g, NT, preferred_element_type=F32)
            ds = (SCALE * p * (dp - delta)).astype(BF16)
            acc_v[n] += jnp.dot(p.astype(BF16), g, preferred_element_type=F32)
            acc_k[n] += jnp.dot(ds, q, preferred_element_type=F32)
            dq = jnp.dot(kt_ref[n], ds, preferred_element_type=F32)
            total = dq if total is None else total + dq
        dq_ref[chip] = total.astype(dq_ref.dtype)

    @pl.when(step == pl.num_programs(0) - 1)
    def _():
        for n, d_ref in enumerate((d1_ref, d2_ref)):
            d_ref[:, :HEAD] = acc_k[n]
            d_ref[:, HEAD:] = acc_v[n]


def tile_call(qg, pair1, pair2, old, after, last):
    first = old is None
    groups, rows, width = qg.shape
    chips = 4
    q_spec = pl.BlockSpec((chips, rows, width), lambda i: (i, 0, 0))
    keys = 2 * ROWS
    kv_spec = pl.BlockSpec((ROWS, width), lambda i: (0, 0))
    sum_spec = pl.BlockSpec((keys, width), lambda i: (0, 0))
    dq_spec = pl.BlockSpec((chips, HEAD, ROWS), lambda i: (i, 0, 0))
    pairs = groups * ROWS * 2 * keys
    return pl.pallas_call(
        functools.partial(tile_kernel, first, chips),
        grid=(groups // chips,),
        in_specs=[q_spec] + [kv_spec] * 4
        + ([] if first else [dq_spec, pl.BlockSpec(memory_space=pl.ANY)]),
        out_specs=[dq_spec, sum_spec, sum_spec],
        out_shape=[
            jax.ShapeDtypeStruct((groups, HEAD, ROWS), BF16 if last else F32),
            jax.ShapeDtypeStruct((keys, width), F32),
            jax.ShapeDtypeStruct((keys, width), F32),
        ],
        scratch_shapes=[
            pltpu.VMEM((2, keys, HEAD), F32),
            pltpu.VMEM((2, keys, HEAD), F32),
            pltpu.VMEM((2, HEAD, keys), BF16),
        ],
        compiler_params=pltpu.CompilerParams(vmem_limit_bytes=40 * 2**20),
        cost_estimate=pl.CostEstimate(
            flops=pairs * HEAD * 20, bytes_accessed=8 * 2**20, transcendentals=pairs
        ),
        name="tile",
    )(*((qg, *pair1, *pair2) if first else (qg, *pair1, *pair2, old, after)))


def shift(x, axis, by):
    n = lax.axis_size(axis)
    return lax.ppermute(x, axis, [(i, (i + by) % n) for i in range(n)])


def local(queries, key_rows, value_rows, attn_output, grad_output, row_lse):
    core = lax.axis_index("core")
    even = core == 0
    mine_q, mine_kv, send, far_kv = pack_call(
        core, queries, key_rows, value_rows, attn_output, grad_output, row_lse
    )
    other = shift(send, "core", 1)
    corners = lax.axis_size("xh") * lax.axis_size("core")
    across = shift(mine_kv, "xh", 1)
    diagonal = lax.ppermute(
        far_kv, ("xh", "core"), [(i, corners - 1 - i) for i in range(corners)]
    )
    near = jnp.concatenate([mine_kv, other[HALF + STATS :]], axis=0)
    peers = math.prod(lax.axis_size(a) for a in GROUP)
    spread, partner = spread_call(peers, mine_q, other, across, diagonal)
    gathered = lax.all_to_all(spread, GROUP, 0, 0, tiled=True)
    keys = {0: [near, partner]}
    for by in (1, 2, 3):
        keys[by] = [shift(x, "z", 1) for x in keys[by - 1]]
        keys[-by] = [shift(x, "z", -1) for x in keys[1 - by]]
    keys[4] = [shift(keys[3][0], "z", 1), shift(keys[-3][1], "z", -1)]

    def low(x):
        return x.astype(BF16)

    total_q, far, own = tile_call(gathered, keys[4], keys[0], None, None, False)
    up = low(far)
    down = None
    after = up
    for by in (3, 2, 1):
        up_in = shift(up, "z", 1)
        down_in = None if down is None else shift(down, "z", -1)
        total_q, du, dd = tile_call(gathered, keys[-by], keys[by], total_q, after, by == 1)
        up = low(du + up_in.astype(F32))
        down = low(dd if down_in is None else dd + down_in.astype(F32))
        after = up
    up_in = shift(up, "z", 1)
    down_in = shift(down, "z", -1)
    returned = lax.all_to_all(total_q, GROUP, 0, 0, tiled=True)
    grad_pair = own + up_in.astype(F32) + down_in.astype(F32)
    grad_kv = grad_pair[:ROWS] + shift(low(grad_pair[ROWS:]), "xh", 1).astype(F32)

    grad_q = jnp.sum(returned.astype(F32), axis=0).T
    grads = jnp.stack([grad_q, grad_kv[:, :HEAD], grad_kv[:, HEAD:]]).astype(BF16)
    kept = grads[:, :HALF]
    moved = shift(grads[:, HALF:], "core", 1)
    out = jnp.concatenate(
        [jnp.where(even, kept, moved), jnp.where(even, moved, kept)], axis=2
    )
    return out[0], out[1], out[2]


def solution(mesh):
    devices = mesh.devices.reshape(4, 2, 8, 2, 2)
    torus = Mesh(devices, AXES)
    rows = P(AXES, None)
    return jax.shard_map(
        local,
        mesh=torus,
        in_specs=(rows, rows, rows, rows, rows, P(None, AXES)),
        out_specs=(rows, rows, rows),
        check_vma=False,
    )
```

```python
import functools
import math

import jax
import jax.numpy as jnp
from jax import lax
from jax.experimental import pallas as pl
from jax.experimental.pallas import tpu as pltpu
from jax.sharding import Mesh, PartitionSpec as P

HEAD = 128
SCALE = HEAD**-0.5
LOG2E = math.log2(math.e)
AXES = ("y", "xh", "z", "xl", "core")
GROUP = ("y", "xl")
ROWS = 256
STATS = 16
HALF = 128
NT = (((1,), (1,)), ((), ()))
F32, BF16 = jnp.float32, jnp.bfloat16


def split3(x):
    hi = x.astype(BF16)
    rest = x - hi.astype(F32)
    mid = rest.astype(BF16)
    low = (rest - mid.astype(F32)).astype(BF16)
    return jnp.concatenate([hi.astype(F32), mid.astype(F32), low.astype(F32)], axis=0)


def pack_kernel(core_ref, q_ref, k_ref, v_ref, o_ref, g_ref, lse_ref, qg_ref, kv_ref, send_ref, far_ref):
    def fill(head, qg, kv):
        cols = slice(head * HEAD, (head + 1) * HEAD)
        g = g_ref[:, cols]
        products = g.astype(F32) * o_ref[:, cols].astype(F32)
        delta = jnp.sum(products.T, axis=0, keepdims=True)
        lse = lse_ref[head : head + 1, :] * LOG2E
        terms = jnp.concatenate([split3(lse), split3(delta)], axis=1)
        terms = jnp.concatenate([terms, jnp.zeros((STATS - 3, 2 * HALF), F32)], axis=0)
        qg[:HALF, :HEAD] = q_ref[:, cols]
        qg[:HALF, HEAD:] = g
        qg[HALF:, :] = terms.astype(BF16)
        kv[:, :HEAD] = k_ref[:, cols]
        kv[:, HEAD:] = v_ref[:, cols]

    send_qg = send_ref.at[: HALF + STATS]
    send_kv = send_ref.at[HALF + STATS :]
    for core in range(2):

        @pl.when(core_ref[0] == core)
        def _():
            fill(core, qg_ref, kv_ref)
            fill(1 - core, send_qg, send_kv)
            far_ref[...] = send_kv[...]


def pack_call(core, *args):
    width = 2 * HEAD
    return pl.pallas_call(
        pack_kernel,
        in_specs=[pl.BlockSpec(memory_space=pltpu.SMEM)]
        + [pl.BlockSpec(memory_space=pltpu.VMEM)] * 6,
        out_specs=[pl.BlockSpec(memory_space=pltpu.VMEM)] * 4,
        out_shape=[
            jax.ShapeDtypeStruct((HALF + STATS, width), BF16),
            jax.ShapeDtypeStruct((HALF, width), BF16),
            jax.ShapeDtypeStruct((2 * HALF + STATS, width), BF16),
            jax.ShapeDtypeStruct((HALF, width), BF16),
        ],
        name="pack",
    )(core.reshape(1), *args)


def spread_kernel(mine_ref, other_ref, _, out_ref):
    rows = HALF + STATS
    for n in range(out_ref.shape[0]):
        out_ref[n, :rows, :] = mine_ref[...]
        out_ref[n, rows:, :] = other_ref[:rows, :]


def spread_call(n, *args):
    return pl.pallas_call(
        spread_kernel,
        in_specs=[pl.BlockSpec(memory_space=pltpu.VMEM)] * 3,
        out_specs=pl.BlockSpec(memory_space=pltpu.VMEM),
        out_shape=jax.ShapeDtypeStruct((n, 2 * (HALF + STATS), 2 * HEAD), BF16),
        name="spread",
    )(*args)


def tile_kernel(first, chips, *refs):
    refs = list(refs)
    qg_ref = refs.pop(0)
    blocks = [(refs.pop(0), refs.pop(0)) for _ in range(2)]
    if not first:
        old_ref = refs.pop(0)
        refs.pop(0)
    dq_ref, d1_ref, d2_ref, acc_k, acc_v, kt_ref = refs
    step = pl.program_id(0)

    def part(block, cols):
        return jnp.concatenate([ref[:, cols] for ref in block], axis=0)

    @pl.when(step == 0)
    def _():
        acc_k[...] = jnp.zeros_like(acc_k)
        acc_v[...] = jnp.zeros_like(acc_v)
        for n, block in enumerate(blocks):
            kt_ref[n] = part(block, slice(0, HEAD)).astype(F32).T.astype(BF16)

    for chip in range(chips):
        qs, gs, lses, deltas = [], [], [], []
        for base in (0, HALF + STATS):
            qs.append(qg_ref[chip, base : base + HALF, :HEAD])
            gs.append(qg_ref[chip, base : base + HALF, HEAD:])
            stats = qg_ref[chip, base + HALF : base + HALF + STATS, :].astype(F32)
            stats = stats[0:1] + stats[1:2] + stats[2:3]
            lses.append(stats[:, :HALF])
            deltas.append(stats[:, HALF:])
        q = jnp.concatenate(qs, axis=0)
        g = jnp.concatenate(gs, axis=0)
        lse = jnp.concatenate(lses, axis=1)
        delta = jnp.concatenate(deltas, axis=1)
        total = None if first else old_ref[chip]
        for n, block in enumerate(blocks):
            k, v = part(block, slice(0, HEAD)), part(block, slice(HEAD, 2 * HEAD))
            s = lax.dot_general(k, q, NT, preferred_element_type=F32)
            p = jnp.exp2(s * (SCALE * LOG2E) - lse)
            dp = lax.dot_general(v, g, NT, preferred_element_type=F32)
            ds = (SCALE * p * (dp - delta)).astype(BF16)
            acc_v[n] += jnp.dot(p.astype(BF16), g, preferred_element_type=F32)
            acc_k[n] += jnp.dot(ds, q, preferred_element_type=F32)
            dq = jnp.dot(kt_ref[n], ds, preferred_element_type=F32)
            total = dq if total is None else total + dq
        dq_ref[chip] = total.astype(dq_ref.dtype)

    @pl.when(step == pl.num_programs(0) - 1)
    def _():
        for n, d_ref in enumerate((d1_ref, d2_ref)):
            d_ref[:, :HEAD] = acc_k[n]
            d_ref[:, HEAD:] = acc_v[n]


def tile_call(qg, pair1, pair2, old, after, last):
    first = old is None
    groups, rows, width = qg.shape
    chips = 4
    q_spec = pl.BlockSpec((chips, rows, width), lambda i: (i, 0, 0))
    keys = 2 * ROWS
    kv_spec = pl.BlockSpec((ROWS, width), lambda i: (0, 0))
    sum_spec = pl.BlockSpec((keys, width), lambda i: (0, 0))
    dq_spec = pl.BlockSpec((chips, HEAD, ROWS), lambda i: (i, 0, 0))
    pairs = groups * ROWS * 2 * keys
    return pl.pallas_call(
        functools.partial(tile_kernel, first, chips),
        grid=(groups // chips,),
        in_specs=[q_spec] + [kv_spec] * 4
        + ([] if first else [dq_spec, pl.BlockSpec(memory_space=pl.ANY)]),
        out_specs=[dq_spec, sum_spec, sum_spec],
        out_shape=[
            jax.ShapeDtypeStruct((groups, HEAD, ROWS), BF16 if last else F32),
            jax.ShapeDtypeStruct((keys, width), F32),
            jax.ShapeDtypeStruct((keys, width), F32),
        ],
        scratch_shapes=[
            pltpu.VMEM((2, keys, HEAD), F32),
            pltpu.VMEM((2, keys, HEAD), F32),
            pltpu.VMEM((2, HEAD, keys), BF16),
        ],
        compiler_params=pltpu.CompilerParams(vmem_limit_bytes=24 * 2**20),
        cost_estimate=pl.CostEstimate(
            flops=pairs * HEAD * 20, bytes_accessed=8 * 2**20, transcendentals=pairs
        ),
        name="tile",
    )(*((qg, *pair1, *pair2) if first else (qg, *pair1, *pair2, old, after)))


def shift(x, axis, by):
    n = lax.axis_size(axis)
    return lax.ppermute(x, axis, [(i, (i + by) % n) for i in range(n)])


def local(queries, key_rows, value_rows, attn_output, grad_output, row_lse):
    core = lax.axis_index("core")
    even = core == 0
    mine_q, mine_kv, send, far_kv = pack_call(
        core, queries, key_rows, value_rows, attn_output, grad_output, row_lse
    )
    other = shift(send, "core", 1)
    corners = lax.axis_size("xh") * lax.axis_size("core")
    across = shift(mine_kv, "xh", 1)
    diagonal = lax.ppermute(
        far_kv, ("xh", "core"), [(i, corners - 1 - i) for i in range(corners)]
    )
    near = jnp.concatenate([mine_kv, other[HALF + STATS :]], axis=0)
    partner = jnp.concatenate([across, diagonal], axis=0)
    keys = {0: [near, partner]}
    for by in (1, 2, 3):
        keys[by] = [shift(x, "z", 1) for x in keys[by - 1]]
        keys[-by] = [shift(x, "z", -1) for x in keys[1 - by]]
    keys[4] = [shift(keys[3][0], "z", 1), shift(keys[-3][1], "z", -1)]
    peers = math.prod(lax.axis_size(a) for a in GROUP)
    spread = spread_call(peers, mine_q, other, keys[1][0])
    gathered = lax.all_to_all(spread, GROUP, 0, 0, tiled=True)

    def low(x):
        return x.astype(BF16)

    total_q, far, own = tile_call(gathered, keys[4], keys[0], None, None, False)
    up = low(far)
    down = None
    after = up
    for by in (3, 2, 1):
        up_in = shift(up, "z", 1)
        down_in = None if down is None else shift(down, "z", -1)
        total_q, du, dd = tile_call(gathered, keys[-by], keys[by], total_q, after, by == 1)
        up = low(du + up_in.astype(F32))
        down = low(dd if down_in is None else dd + down_in.astype(F32))
        after = up
    up_in = shift(up, "z", 1)
    down_in = shift(down, "z", -1)
    returned = lax.all_to_all(total_q, GROUP, 0, 0, tiled=True)
    grad_pair = own + up_in.astype(F32) + down_in.astype(F32)
    grad_kv = grad_pair[:ROWS] + shift(low(grad_pair[ROWS:]), "xh", 1).astype(F32)

    grad_q = jnp.sum(returned.astype(F32), axis=0).T
    grads = jnp.stack([grad_q, grad_kv[:, :HEAD], grad_kv[:, HEAD:]]).astype(BF16)
    kept = grads[:, :HALF]
    moved = shift(grads[:, HALF:], "core", 1)
    out = jnp.concatenate(
        [jnp.where(even, kept, moved), jnp.where(even, moved, kept)], axis=2
    )
    return out[0], out[1], out[2]


def solution(mesh):
    devices = mesh.devices.reshape(4, 2, 8, 2, 2)
    torus = Mesh(devices, AXES)
    rows = P(AXES, None)
    return jax.shard_map(
        local,
        mesh=torus,
        in_specs=(rows, rows, rows, rows, rows, P(None, AXES)),
        out_specs=(rows, rows, rows),
        check_vma=False,
    )
```

```python
import functools
import math

import jax
import jax.numpy as jnp
from jax import lax
from jax.experimental import pallas as pl
from jax.experimental.pallas import tpu as pltpu
from jax.sharding import Mesh, PartitionSpec as P

HEAD = 128
SCALE = HEAD**-0.5
LOG2E = math.log2(math.e)
AXES = ("y", "xh", "z", "xl", "core")
GROUP = ("y", "xl")
ROWS = 256
STATS = 16
HALF = 128
NT = (((1,), (1,)), ((), ()))
F32, BF16 = jnp.float32, jnp.bfloat16


def split3(x):
    hi = x.astype(BF16)
    rest = x - hi.astype(F32)
    mid = rest.astype(BF16)
    low = (rest - mid.astype(F32)).astype(BF16)
    return jnp.concatenate([hi.astype(F32), mid.astype(F32), low.astype(F32)], axis=0)


def pack_kernel(core_ref, q_ref, k_ref, v_ref, o_ref, g_ref, lse_ref, qg_ref, kv_ref, send_ref, far_ref):
    def fill(head, qg, kv):
        cols = slice(head * HEAD, (head + 1) * HEAD)
        g = g_ref[:, cols]
        products = g.astype(F32) * o_ref[:, cols].astype(F32)
        delta = jnp.sum(products.T, axis=0, keepdims=True)
        lse = lse_ref[head : head + 1, :] * LOG2E
        terms = jnp.concatenate([split3(lse), split3(delta)], axis=1)
        terms = jnp.concatenate([terms, jnp.zeros((STATS - 3, 2 * HALF), F32)], axis=0)
        qg[:HALF, :HEAD] = q_ref[:, cols]
        qg[:HALF, HEAD:] = g
        qg[HALF:, :] = terms.astype(BF16)
        kv[:, :HEAD] = k_ref[:, cols]
        kv[:, HEAD:] = v_ref[:, cols]

    send_qg = send_ref.at[: HALF + STATS]
    send_kv = send_ref.at[HALF + STATS :]
    for core in range(2):

        @pl.when(core_ref[0] == core)
        def _():
            fill(core, qg_ref, kv_ref)
            fill(1 - core, send_qg, send_kv)
            far_ref[...] = send_kv[...]


def pack_call(core, *args):
    width = 2 * HEAD
    return pl.pallas_call(
        pack_kernel,
        in_specs=[pl.BlockSpec(memory_space=pltpu.SMEM)]
        + [pl.BlockSpec(memory_space=pltpu.VMEM)] * 6,
        out_specs=[pl.BlockSpec(memory_space=pltpu.VMEM)] * 4,
        out_shape=[
            jax.ShapeDtypeStruct((HALF + STATS, width), BF16),
            jax.ShapeDtypeStruct((HALF, width), BF16),
            jax.ShapeDtypeStruct((2 * HALF + STATS, width), BF16),
            jax.ShapeDtypeStruct((HALF, width), BF16),
        ],
        name="pack",
    )(core.reshape(1), *args)


def spread_kernel(mine_ref, other_ref, _a, _b, out_ref):
    rows = HALF + STATS
    for n in range(out_ref.shape[0]):
        out_ref[n, :rows, :] = mine_ref[...]
        out_ref[n, rows:, :] = other_ref[:rows, :]


def spread_call(n, *args):
    return pl.pallas_call(
        spread_kernel,
        in_specs=[pl.BlockSpec(memory_space=pltpu.VMEM)] * 4,
        out_specs=pl.BlockSpec(memory_space=pltpu.VMEM),
        out_shape=jax.ShapeDtypeStruct((n, 2 * (HALF + STATS), 2 * HEAD), BF16),
        name="spread",
    )(*args)


def tile_kernel(first, chips, *refs):
    refs = list(refs)
    qg_ref = refs.pop(0)
    blocks = [(refs.pop(0), refs.pop(0)) for _ in range(2)]
    if not first:
        old_ref = refs.pop(0)
        refs.pop(0)
    dq_ref, d1_ref, d2_ref, acc_k, acc_v, kt_ref = refs
    step = pl.program_id(0)

    def part(block, cols):
        return jnp.concatenate([ref[:, cols] for ref in block], axis=0)

    @pl.when(step == 0)
    def _():
        acc_k[...] = jnp.zeros_like(acc_k)
        acc_v[...] = jnp.zeros_like(acc_v)
        for n, block in enumerate(blocks):
            kt_ref[n] = part(block, slice(0, HEAD)).astype(F32).T.astype(BF16)

    for chip in range(chips):
        qs, gs, lses, deltas = [], [], [], []
        for base in (0, HALF + STATS):
            qs.append(qg_ref[chip, base : base + HALF, :HEAD])
            gs.append(qg_ref[chip, base : base + HALF, HEAD:])
            stats = qg_ref[chip, base + HALF : base + HALF + STATS, :].astype(F32)
            stats = stats[0:1] + stats[1:2] + stats[2:3]
            lses.append(stats[:, :HALF])
            deltas.append(stats[:, HALF:])
        q = jnp.concatenate(qs, axis=0)
        g = jnp.concatenate(gs, axis=0)
        lse = jnp.concatenate(lses, axis=1)
        delta = jnp.concatenate(deltas, axis=1)
        total = None if first else old_ref[chip]
        for n, block in enumerate(blocks):
            k, v = part(block, slice(0, HEAD)), part(block, slice(HEAD, 2 * HEAD))
            s = lax.dot_general(k, q, NT, preferred_element_type=F32)
            p = jnp.exp2(s * (SCALE * LOG2E) - lse)
            dp = lax.dot_general(v, g, NT, preferred_element_type=F32)
            ds = (SCALE * p * (dp - delta)).astype(BF16)
            acc_v[n] += jnp.dot(p.astype(BF16), g, preferred_element_type=F32)
            acc_k[n] += jnp.dot(ds, q, preferred_element_type=F32)
            dq = jnp.dot(kt_ref[n], ds, preferred_element_type=F32)
            total = dq if total is None else total + dq
        dq_ref[chip] = total.astype(dq_ref.dtype)

    @pl.when(step == pl.num_programs(0) - 1)
    def _():
        for n, d_ref in enumerate((d1_ref, d2_ref)):
            d_ref[:, :HEAD] = acc_k[n]
            d_ref[:, HEAD:] = acc_v[n]


def tile_call(qg, pair1, pair2, old, after, last):
    first = old is None
    groups, rows, width = qg.shape
    chips = 4
    q_spec = pl.BlockSpec((chips, rows, width), lambda i: (i, 0, 0))
    keys = 2 * ROWS
    kv_spec = pl.BlockSpec((ROWS, width), lambda i: (0, 0))
    sum_spec = pl.BlockSpec((keys, width), lambda i: (0, 0))
    dq_spec = pl.BlockSpec((chips, HEAD, ROWS), lambda i: (i, 0, 0))
    pairs = groups * ROWS * 2 * keys
    return pl.pallas_call(
        functools.partial(tile_kernel, first, chips),
        grid=(groups // chips,),
        in_specs=[q_spec] + [kv_spec] * 4
        + ([] if first else [dq_spec, pl.BlockSpec(memory_space=pl.ANY)]),
        out_specs=[dq_spec, sum_spec, sum_spec],
        out_shape=[
            jax.ShapeDtypeStruct((groups, HEAD, ROWS), BF16 if last else F32),
            jax.ShapeDtypeStruct((keys, width), F32),
            jax.ShapeDtypeStruct((keys, width), F32),
        ],
        scratch_shapes=[
            pltpu.VMEM((2, keys, HEAD), F32),
            pltpu.VMEM((2, keys, HEAD), F32),
            pltpu.VMEM((2, HEAD, keys), BF16),
        ],
        compiler_params=pltpu.CompilerParams(vmem_limit_bytes=24 * 2**20),
        cost_estimate=pl.CostEstimate(
            flops=pairs * HEAD * 20, bytes_accessed=8 * 2**20, transcendentals=pairs
        ),
        name="tile",
    )(*((qg, *pair1, *pair2) if first else (qg, *pair1, *pair2, old, after)))


def shift(x, axis, by):
    n = lax.axis_size(axis)
    return lax.ppermute(x, axis, [(i, (i + by) % n) for i in range(n)])


def local(queries, key_rows, value_rows, attn_output, grad_output, row_lse):
    core = lax.axis_index("core")
    even = core == 0
    mine_q, mine_kv, send, far_kv = pack_call(
        core, queries, key_rows, value_rows, attn_output, grad_output, row_lse
    )
    other = shift(send, "core", 1)
    corners = lax.axis_size("xh") * lax.axis_size("core")
    across = shift(mine_kv, "xh", 1)
    diagonal = lax.ppermute(
        far_kv, ("xh", "core"), [(i, corners - 1 - i) for i in range(corners)]
    )
    near = jnp.concatenate([mine_kv, other[HALF + STATS :]], axis=0)
    partner = jnp.concatenate([across, diagonal], axis=0)
    keys = {0: [near, partner]}
    for by in (1, 2, 3):
        keys[by] = [shift(x, "z", 1) for x in keys[by - 1]]
        keys[-by] = [shift(x, "z", -1) for x in keys[1 - by]]
    keys[4] = [shift(keys[3][0], "z", 1), shift(keys[-3][1], "z", -1)]
    peers = math.prod(lax.axis_size(a) for a in GROUP)
    spread = spread_call(peers, mine_q, other, keys[1][1], keys[-1][1])
    gathered = lax.all_to_all(spread, GROUP, 0, 0, tiled=True)

    def low(x):
        return x.astype(BF16)

    total_q, far, own = tile_call(gathered, keys[4], keys[0], None, None, False)
    up = low(far)
    down = None
    after = up
    for by in (3, 2, 1):
        up_in = shift(up, "z", 1)
        down_in = None if down is None else shift(down, "z", -1)
        total_q, du, dd = tile_call(gathered, keys[-by], keys[by], total_q, after, by == 1)
        up = low(du + up_in.astype(F32))
        down = low(dd if down_in is None else dd + down_in.astype(F32))
        after = up
    up_in = shift(up, "z", 1)
    down_in = shift(down, "z", -1)
    returned = lax.all_to_all(total_q, GROUP, 0, 0, tiled=True)
    grad_pair = own + up_in.astype(F32) + down_in.astype(F32)
    grad_kv = grad_pair[:ROWS] + shift(low(grad_pair[ROWS:]), "xh", 1).astype(F32)

    grad_q = jnp.sum(returned.astype(F32), axis=0).T
    grads = jnp.stack([grad_q, grad_kv[:, :HEAD], grad_kv[:, HEAD:]]).astype(BF16)
    kept = grads[:, :HALF]
    moved = shift(grads[:, HALF:], "core", 1)
    out = jnp.concatenate(
        [jnp.where(even, kept, moved), jnp.where(even, moved, kept)], axis=2
    )
    return out[0], out[1], out[2]


def solution(mesh):
    devices = mesh.devices.reshape(4, 2, 8, 2, 2)
    torus = Mesh(devices, AXES)
    rows = P(AXES, None)
    return jax.shard_map(
        local,
        mesh=torus,
        in_specs=(rows, rows, rows, rows, rows, P(None, AXES)),
        out_specs=(rows, rows, rows),
        check_vma=False,
    )
```

```python
import functools
import math

import jax
import jax.numpy as jnp
from jax import lax
from jax.experimental import pallas as pl
from jax.experimental.pallas import tpu as pltpu
from jax.sharding import Mesh, PartitionSpec as P

HEAD = 128
SCALE = HEAD**-0.5
LOG2E = math.log2(math.e)
AXES = ("y", "xh", "z", "xl", "core")
GROUP = ("y", "xl")
ROWS = 256
STATS = 16
HALF = 128
NT = (((1,), (1,)), ((), ()))
F32, BF16 = jnp.float32, jnp.bfloat16


def split3(x):
    hi = x.astype(BF16)
    rest = x - hi.astype(F32)
    mid = rest.astype(BF16)
    low = (rest - mid.astype(F32)).astype(BF16)
    return jnp.concatenate([hi.astype(F32), mid.astype(F32), low.astype(F32)], axis=0)


def pack_kernel(core_ref, q_ref, k_ref, v_ref, o_ref, g_ref, lse_ref, qg_ref, kv_ref, send_ref):
    def fill(head, qg, kv):
        cols = slice(head * HEAD, (head + 1) * HEAD)
        g = g_ref[:, cols]
        products = g.astype(F32) * o_ref[:, cols].astype(F32)
        delta = jnp.sum(products.T, axis=0, keepdims=True)
        lse = lse_ref[head : head + 1, :] * LOG2E
        terms = jnp.concatenate([split3(lse), split3(delta)], axis=1)
        terms = jnp.concatenate([terms, jnp.zeros((STATS - 3, 2 * HALF), F32)], axis=0)
        qg[:HALF, :HEAD] = q_ref[:, cols]
        qg[:HALF, HEAD:] = g
        qg[HALF:, :] = terms.astype(BF16)
        kv[:, :HEAD] = k_ref[:, cols]
        kv[:, HEAD:] = v_ref[:, cols]

    send_qg = send_ref.at[: HALF + STATS]
    send_kv = send_ref.at[HALF + STATS :]
    for core in range(2):

        @pl.when(core_ref[0] == core)
        def _():
            fill(core, qg_ref, kv_ref)
            fill(1 - core, send_qg, send_kv)


def pack_call(core, *args):
    width = 2 * HEAD
    return pl.pallas_call(
        pack_kernel,
        in_specs=[pl.BlockSpec(memory_space=pltpu.SMEM)]
        + [pl.BlockSpec(memory_space=pltpu.VMEM)] * 6,
        out_specs=[pl.BlockSpec(memory_space=pltpu.VMEM)] * 3,
        out_shape=[
            jax.ShapeDtypeStruct((HALF + STATS, width), BF16),
            jax.ShapeDtypeStruct((HALF, width), BF16),
            jax.ShapeDtypeStruct((2 * HALF + STATS, width), BF16),
        ],
        name="pack",
    )(core.reshape(1), *args)


def spread_kernel(mine_ref, kv_ref, other_ref, out_ref, keys_ref):
    rows = HALF + STATS
    for n in range(out_ref.shape[0]):
        out_ref[n, :rows, :] = mine_ref[...]
        out_ref[n, rows:, :] = other_ref[:rows, :]
    keys_ref[:HALF, :] = kv_ref[...]
    keys_ref[HALF:, :] = other_ref[rows:, :]


def spread_call(n, *args):
    return pl.pallas_call(
        spread_kernel,
        in_specs=[pl.BlockSpec(memory_space=pltpu.VMEM)] * 3,
        out_specs=[pl.BlockSpec(memory_space=pltpu.VMEM)] * 2,
        out_shape=[
            jax.ShapeDtypeStruct((n, 2 * (HALF + STATS), 2 * HEAD), BF16),
            jax.ShapeDtypeStruct((ROWS, 2 * HEAD), BF16),
        ],
        name="spread",
    )(*args)


def tile_kernel(count, first, waits, chips, *refs):
    refs = list(refs)
    qg_ref = refs.pop(0)
    blocks = [refs.pop(0) for _ in range(count)]
    if not first:
        old_ref = refs.pop(0)
    if waits:
        refs.pop(0)
    dq_ref = refs.pop(0)
    sums = [refs.pop(0) for _ in range(count)]
    acc_k, acc_v, kt_ref = refs
    step = pl.program_id(0)

    @pl.when(step == 0)
    def _():
        acc_k[...] = jnp.zeros_like(acc_k)
        acc_v[...] = jnp.zeros_like(acc_v)
        for n, kv_ref in enumerate(blocks):
            kt_ref[n] = kv_ref[:, :HEAD].astype(F32).T.astype(BF16)

    for chip in range(chips):
        qs, gs, lses, deltas = [], [], [], []
        for base in (0, HALF + STATS):
            qs.append(qg_ref[chip, base : base + HALF, :HEAD])
            gs.append(qg_ref[chip, base : base + HALF, HEAD:])
            stats = qg_ref[chip, base + HALF : base + HALF + STATS, :].astype(F32)
            stats = stats[0:1] + stats[1:2] + stats[2:3]
            lses.append(stats[:, :HALF])
            deltas.append(stats[:, HALF:])
        q = jnp.concatenate(qs, axis=0)
        g = jnp.concatenate(gs, axis=0)
        lse = jnp.concatenate(lses, axis=1)
        delta = jnp.concatenate(deltas, axis=1)
        total = None if first else old_ref[chip]
        for n, kv_ref in enumerate(blocks):
            s = lax.dot_general(kv_ref[:, :HEAD], q, NT, preferred_element_type=F32)
            p = jnp.exp2(s * (SCALE * LOG2E) - lse)
            dp = lax.dot_general(kv_ref[:, HEAD:], g, NT, preferred_element_type=F32)
            ds = (SCALE * p * (dp - delta)).astype(BF16)
            acc_v[n] += jnp.dot(p.astype(BF16), g, preferred_element_type=F32)
            acc_k[n] += jnp.dot(ds, q, preferred_element_type=F32)
            dq = jnp.dot(kt_ref[n], ds, preferred_element_type=F32)
            total = dq if total is None else total + dq
        dq_ref[chip] = total.astype(dq_ref.dtype)

    @pl.when(step == pl.num_programs(0) - 1)
    def _():
        for n, d_ref in enumerate(sums):
            d_ref[:, :HEAD] = acc_k[n]
            d_ref[:, HEAD:] = acc_v[n]


def tile_call(qg, blocks, old=None, after=None, last=False):
    first = old is None
    groups, rows, width = qg.shape
    count, keys = len(blocks), blocks[0].shape[0]
    chips = 4
    q_spec = pl.BlockSpec((chips, rows, width), lambda i: (i, 0, 0))
    kv_spec = pl.BlockSpec((keys, width), lambda i: (0, 0))
    dq_spec = pl.BlockSpec((chips, HEAD, ROWS), lambda i: (i, 0, 0))
    dq_shape = jax.ShapeDtypeStruct((groups, HEAD, ROWS), BF16 if last else F32)
    args, specs = [qg, *blocks], [q_spec] + [kv_spec] * count
    if not first:
        args.append(old)
        specs.append(dq_spec)
    if after is not None:
        args.append(after)
        specs.append(pl.BlockSpec(memory_space=pl.ANY))
    pairs = groups * ROWS * count * keys
    return pl.pallas_call(
        functools.partial(tile_kernel, count, first, after is not None, chips),
        grid=(groups // chips,),
        in_specs=specs,
        out_specs=[dq_spec] + [kv_spec] * count,
        out_shape=[dq_shape] + [jax.ShapeDtypeStruct((keys, width), F32)] * count,
        scratch_shapes=[
            pltpu.VMEM((count, keys, HEAD), F32),
            pltpu.VMEM((count, keys, HEAD), F32),
            pltpu.VMEM((count, HEAD, keys), BF16),
        ],
        compiler_params=pltpu.CompilerParams(vmem_limit_bytes=40 * 2**20),
        cost_estimate=pl.CostEstimate(
            flops=pairs * HEAD * 20, bytes_accessed=8 * 2**20, transcendentals=pairs
        ),
        name="tile",
    )(*args)


def shift(x, axis, by):
    n = lax.axis_size(axis)
    return lax.ppermute(x, axis, [(i, (i + by) % n) for i in range(n)])


def local(queries, key_rows, value_rows, attn_output, grad_output, row_lse):
    core = lax.axis_index("core")
    even = core == 0
    mine_q, mine_kv, send = pack_call(
        core, queries, key_rows, value_rows, attn_output, grad_output, row_lse
    )
    other = shift(send, "core", 1)
    peers = math.prod(lax.axis_size(a) for a in GROUP)
    spread, key_pack = spread_call(peers, mine_q, mine_kv, other)
    key_pair = jnp.concatenate([key_pack, shift(key_pack, "xh", 1)], axis=0)
    gathered = lax.all_to_all(spread, GROUP, 0, 0, tiled=True)
    keys = {0: key_pair}
    for by in (1, 2, 3):
        keys[by] = shift(keys[by - 1], "z", 1)
        keys[-by] = shift(keys[1 - by], "z", -1)
    total_q, own = tile_call(gathered, [keys[0]])
    zero = jnp.minimum(jnp.abs(own[0, 0]), 0.0).astype(BF16)
    keys[4] = jnp.concatenate(
        [shift(keys[3][:ROWS] + zero, "z", 1), shift(keys[-3][ROWS:] + zero, "z", -1)],
        axis=0,
    )

    def low(x):
        return x.astype(BF16)

    total_q, far = tile_call(gathered, [keys[4]], total_q)
    up = low(far)
    down = None
    after = up
    for by in (3, 2):
        up_in = shift(up, "z", 1)
        down_in = None if down is None else shift(down, "z", -1)
        total_q, du, dd = tile_call(gathered, [keys[-by], keys[by]], total_q, after)
        up = low(du + up_in.astype(F32))
        down = low(dd if down_in is None else dd + down_in.astype(F32))
        after = up
    up_in = shift(up, "z", 1)
    down_in = shift(down, "z", -1)
    total_q, dd = tile_call(gathered, [keys[1]], total_q, after)
    down = low(dd + down_in.astype(F32))
    down_in = shift(down, "z", -1)
    total_q, du = tile_call(gathered, [keys[-1]], total_q, down, True)
    up = low(du + up_in.astype(F32))
    up_in = shift(up, "z", 1)
    returned = lax.all_to_all(total_q, GROUP, 0, 0, tiled=True)
    grad_pair = own + up_in.astype(F32) + down_in.astype(F32)
    grad_kv = grad_pair[:ROWS] + shift(low(grad_pair[ROWS:]), "xh", 1).astype(F32)

    grad_q = jnp.sum(returned.astype(F32), axis=0).T
    grads = jnp.stack([grad_q, grad_kv[:, :HEAD], grad_kv[:, HEAD:]]).astype(BF16)
    kept = grads[:, :HALF]
    moved = shift(grads[:, HALF:], "core", 1)
    out = jnp.concatenate(
        [jnp.where(even, kept, moved), jnp.where(even, moved, kept)], axis=2
    )
    return out[0], out[1], out[2]


def solution(mesh):
    devices = mesh.devices.reshape(4, 2, 8, 2, 2)
    torus = Mesh(devices, AXES)
    rows = P(AXES, None)
    return jax.shard_map(
        local,
        mesh=torus,
        in_specs=(rows, rows, rows, rows, rows, P(None, AXES)),
        out_specs=(rows, rows, rows),
        check_vma=False,
    )
```

```python
import functools
import math

import jax
import jax.numpy as jnp
from jax import lax
from jax.experimental import pallas as pl
from jax.experimental.pallas import tpu as pltpu
from jax.sharding import Mesh, PartitionSpec as P

HEAD = 128
SCALE = HEAD**-0.5
LOG2E = math.log2(math.e)
AXES = ("y", "xh", "z", "xl", "core")
GROUP = ("y", "xl")
ROWS = 256
STATS = 16
HALF = 128
NT = (((1,), (1,)), ((), ()))
F32, BF16 = jnp.float32, jnp.bfloat16


def split3(x):
    hi = x.astype(BF16)
    rest = x - hi.astype(F32)
    mid = rest.astype(BF16)
    low = (rest - mid.astype(F32)).astype(BF16)
    return jnp.concatenate([hi.astype(F32), mid.astype(F32), low.astype(F32)], axis=0)


def pack_kernel(core_ref, q_ref, k_ref, v_ref, o_ref, g_ref, lse_ref, qg_ref, kv_ref, send_ref):
    def fill(head, qg, kv):
        cols = slice(head * HEAD, (head + 1) * HEAD)
        g = g_ref[:, cols]
        products = g.astype(F32) * o_ref[:, cols].astype(F32)
        delta = jnp.sum(products.T, axis=0, keepdims=True)
        lse = lse_ref[head : head + 1, :] * LOG2E
        terms = jnp.concatenate([split3(lse), split3(delta)], axis=1)
        terms = jnp.concatenate([terms, jnp.zeros((STATS - 3, 2 * HALF), F32)], axis=0)
        qg[:HALF, :HEAD] = q_ref[:, cols]
        qg[:HALF, HEAD:] = g
        qg[HALF:, :] = terms.astype(BF16)
        kv[:, :HEAD] = k_ref[:, cols]
        kv[:, HEAD:] = v_ref[:, cols]

    send_qg = send_ref.at[: HALF + STATS]
    send_kv = send_ref.at[HALF + STATS :]
    for core in range(2):

        @pl.when(core_ref[0] == core)
        def _():
            fill(core, qg_ref, kv_ref)
            fill(1 - core, send_qg, send_kv)


def pack_call(core, *args):
    width = 2 * HEAD
    return pl.pallas_call(
        pack_kernel,
        in_specs=[pl.BlockSpec(memory_space=pltpu.SMEM)]
        + [pl.BlockSpec(memory_space=pltpu.VMEM)] * 6,
        out_specs=[pl.BlockSpec(memory_space=pltpu.VMEM)] * 3,
        out_shape=[
            jax.ShapeDtypeStruct((HALF + STATS, width), BF16),
            jax.ShapeDtypeStruct((HALF, width), BF16),
            jax.ShapeDtypeStruct((2 * HALF + STATS, width), BF16),
        ],
        name="pack",
    )(core.reshape(1), *args)


def spread_kernel(mine_ref, kv_ref, other_ref, out_ref, keys_ref):
    rows = HALF + STATS
    for n in range(out_ref.shape[0]):
        out_ref[n, :rows, :] = mine_ref[...]
        out_ref[n, rows:, :] = other_ref[:rows, :]
    keys_ref[:HALF, :] = kv_ref[...]
    keys_ref[HALF:, :] = other_ref[rows:, :]


def spread_call(n, *args):
    return pl.pallas_call(
        spread_kernel,
        in_specs=[pl.BlockSpec(memory_space=pltpu.VMEM)] * 3,
        out_specs=[pl.BlockSpec(memory_space=pltpu.VMEM)] * 2,
        out_shape=[
            jax.ShapeDtypeStruct((n, 2 * (HALF + STATS), 2 * HEAD), BF16),
            jax.ShapeDtypeStruct((ROWS, 2 * HEAD), BF16),
        ],
        name="spread",
    )(*args)


def tile_kernel(first, chips, *refs):
    if first:
        qg_ref, kv1_ref, kv2_ref, dq_ref, d1_ref, d2_ref, acc_k, acc_v, kt_ref = refs
    else:
        qg_ref, kv1_ref, kv2_ref, old_ref, _, dq_ref, d1_ref, d2_ref, acc_k, acc_v, kt_ref = refs
    step = pl.program_id(0)
    blocks = (kv1_ref, kv2_ref)

    @pl.when(step == 0)
    def _():
        acc_k[...] = jnp.zeros_like(acc_k)
        acc_v[...] = jnp.zeros_like(acc_v)
        for n, kv_ref in enumerate(blocks):
            kt_ref[n] = kv_ref[:, :HEAD].astype(F32).T.astype(BF16)

    for chip in range(chips):
        qs, gs, lses, deltas = [], [], [], []
        for base in (0, HALF + STATS):
            qs.append(qg_ref[chip, base : base + HALF, :HEAD])
            gs.append(qg_ref[chip, base : base + HALF, HEAD:])
            stats = qg_ref[chip, base + HALF : base + HALF + STATS, :].astype(F32)
            stats = stats[0:1] + stats[1:2] + stats[2:3]
            lses.append(stats[:, :HALF])
            deltas.append(stats[:, HALF:])
        q = jnp.concatenate(qs, axis=0)
        g = jnp.concatenate(gs, axis=0)
        lse = jnp.concatenate(lses, axis=1)
        delta = jnp.concatenate(deltas, axis=1)
        total = None if first else old_ref[chip]
        for n, kv_ref in enumerate(blocks):
            s = lax.dot_general(kv_ref[:, :HEAD], q, NT, preferred_element_type=F32)
            p = jnp.exp2(s * (SCALE * LOG2E) - lse)
            dp = lax.dot_general(kv_ref[:, HEAD:], g, NT, preferred_element_type=F32)
            ds = (SCALE * p * (dp - delta)).astype(BF16)
            acc_v[n] += jnp.dot(p.astype(BF16), g, preferred_element_type=F32)
            acc_k[n] += jnp.dot(ds, q, preferred_element_type=F32)
            dq = jnp.dot(kt_ref[n], ds, preferred_element_type=F32)
            total = dq if total is None else total + dq
        dq_ref[chip] = total.astype(dq_ref.dtype)

    @pl.when(step == pl.num_programs(0) - 1)
    def _():
        for n, d_ref in enumerate((d1_ref, d2_ref)):
            d_ref[:, :HEAD] = acc_k[n]
            d_ref[:, HEAD:] = acc_v[n]


def tile_call(qg, kv1, kv2, old, after, last):
    first = old is None
    groups, rows, width = qg.shape
    chips = 4
    q_spec = pl.BlockSpec((chips, rows, width), lambda i: (i, 0, 0))
    keys = kv1.shape[0]
    kv_spec = pl.BlockSpec((keys, width), lambda i: (0, 0))
    dq_spec = pl.BlockSpec((chips, HEAD, ROWS), lambda i: (i, 0, 0))
    pairs = groups * ROWS * 2 * keys
    return pl.pallas_call(
        functools.partial(tile_kernel, first, chips),
        grid=(groups // chips,),
        in_specs=[q_spec, kv_spec, kv_spec]
        + ([] if first else [dq_spec, pl.BlockSpec(memory_space=pl.ANY)]),
        out_specs=[dq_spec, kv_spec, kv_spec],
        out_shape=[
            jax.ShapeDtypeStruct((groups, HEAD, ROWS), BF16 if last else F32),
            jax.ShapeDtypeStruct((keys, width), F32),
            jax.ShapeDtypeStruct((keys, width), F32),
        ],
        scratch_shapes=[
            pltpu.VMEM((2, keys, HEAD), F32),
            pltpu.VMEM((2, keys, HEAD), F32),
            pltpu.VMEM((2, HEAD, keys), BF16),
        ],
        compiler_params=pltpu.CompilerParams(vmem_limit_bytes=40 * 2**20),
        cost_estimate=pl.CostEstimate(
            flops=pairs * HEAD * 20, bytes_accessed=8 * 2**20, transcendentals=pairs
        ),
        name="tile",
    )(*((qg, kv1, kv2) if first else (qg, kv1, kv2, old, after)))


def shift(x, axis, by):
    n = lax.axis_size(axis)
    return lax.ppermute(x, axis, [(i, (i + by) % n) for i in range(n)])


def local(queries, key_rows, value_rows, attn_output, grad_output, row_lse):
    core = lax.axis_index("core")
    even = core == 0
    mine_q, mine_kv, send = pack_call(
        core, queries, key_rows, value_rows, attn_output, grad_output, row_lse
    )
    other = shift(send, "core", 1)
    peers = math.prod(lax.axis_size(a) for a in GROUP)
    spread, key_pack = spread_call(peers, mine_q, mine_kv, other)
    key_pair = jnp.concatenate([key_pack, shift(key_pack, "xh", 1)], axis=0)
    gathered = lax.all_to_all(spread, GROUP, 0, 0, tiled=True)
    keys = {0: key_pair}
    for by in (1, 2, 3):
        keys[by] = shift(keys[by - 1], "z", 1)
        keys[-by] = shift(keys[1 - by], "z", -1)
    keys[4] = jnp.concatenate(
        [shift(keys[3][:ROWS], "z", 1), shift(keys[-3][ROWS:], "z", -1)], axis=0
    )

    def low(x):
        return x.astype(BF16)

    total_q, du, dd = tile_call(gathered, keys[-3], keys[3], None, None, False)
    up, down = low(du), low(dd)
    up_in, down_in = shift(up, "z", 1), shift(down, "z", -1)
    total_q, far, own = tile_call(gathered, keys[4], keys[0], total_q, up, False)
    far = low(far)
    after = far
    for by in (2, 1):
        total_q, du, dd = tile_call(gathered, keys[-by], keys[by], total_q, after, by == 1)
        up, down = low(du + up_in.astype(F32)), low(dd + down_in.astype(F32))
        up_in, down_in = shift(up, "z", 1), shift(down, "z", -1)
        after = up
    far_in = shift(far, "z", 4)
    returned = lax.all_to_all(total_q, GROUP, 0, 0, tiled=True)
    grad_pair = own + far_in.astype(F32) + up_in.astype(F32) + down_in.astype(F32)
    grad_kv = grad_pair[:ROWS] + shift(low(grad_pair[ROWS:]), "xh", 1).astype(F32)

    grad_q = jnp.sum(returned.astype(F32), axis=0).T
    grads = jnp.stack([grad_q, grad_kv[:, :HEAD], grad_kv[:, HEAD:]]).astype(BF16)
    kept = grads[:, :HALF]
    moved = shift(grads[:, HALF:], "core", 1)
    out = jnp.concatenate(
        [jnp.where(even, kept, moved), jnp.where(even, moved, kept)], axis=2
    )
    return out[0], out[1], out[2]


def solution(mesh):
    devices = mesh.devices.reshape(4, 2, 8, 2, 2)
    torus = Mesh(devices, AXES)
    rows = P(AXES, None)
    return jax.shard_map(
        local,
        mesh=torus,
        in_specs=(rows, rows, rows, rows, rows, P(None, AXES)),
        out_specs=(rows, rows, rows),
        check_vma=False,
    )
```

```python
import functools
import math

import jax
import jax.numpy as jnp
from jax import lax
from jax.experimental import pallas as pl
from jax.experimental.pallas import tpu as pltpu
from jax.sharding import Mesh, PartitionSpec as P

HEAD = 128
SCALE = HEAD**-0.5
LOG2E = math.log2(math.e)
AXES = ("y", "xh", "z", "xl", "core")
GROUP = ("y", "xl")
ROWS = 256
STATS = 16
HALF = 128
NT = (((1,), (1,)), ((), ()))
F32, BF16 = jnp.float32, jnp.bfloat16


def split3(x):
    hi = x.astype(BF16)
    rest = x - hi.astype(F32)
    mid = rest.astype(BF16)
    low = (rest - mid.astype(F32)).astype(BF16)
    return jnp.concatenate([hi.astype(F32), mid.astype(F32), low.astype(F32)], axis=0)


def pack_kernel(core_ref, q_ref, k_ref, v_ref, o_ref, g_ref, lse_ref, mine_ref, send_ref):
    def fill(head, qg, kv):
        cols = slice(head * HEAD, (head + 1) * HEAD)
        g = g_ref[:, cols]
        products = g.astype(F32) * o_ref[:, cols].astype(F32)
        delta = jnp.sum(products.T, axis=0, keepdims=True)
        lse = lse_ref[head : head + 1, :] * LOG2E
        terms = jnp.concatenate([split3(lse), split3(delta)], axis=1)
        terms = jnp.concatenate([terms, jnp.zeros((STATS - 3, 2 * HALF), F32)], axis=0)
        qg[:HALF, :HEAD] = q_ref[:, cols]
        qg[:HALF, HEAD:] = g
        qg[HALF:, :] = terms.astype(BF16)
        kv[:, :HEAD] = k_ref[:, cols]
        kv[:, HEAD:] = v_ref[:, cols]

    def halves(ref):
        return ref.at[: HALF + STATS], ref.at[HALF + STATS :]

    for core in range(2):

        @pl.when(core_ref[0] == core)
        def _():
            fill(core, *halves(mine_ref))
            fill(1 - core, *halves(send_ref))


def pack_call(core, *args):
    width = 2 * HEAD
    return pl.pallas_call(
        pack_kernel,
        in_specs=[pl.BlockSpec(memory_space=pltpu.SMEM)]
        + [pl.BlockSpec(memory_space=pltpu.VMEM)] * 6,
        out_specs=[pl.BlockSpec(memory_space=pltpu.VMEM)] * 2,
        out_shape=[jax.ShapeDtypeStruct((2 * HALF + STATS, width), BF16)] * 2,
        name="pack",
    )(core.reshape(1), *args)


def spread_kernel(mine_ref, other_ref, out_ref, keys_ref):
    rows = HALF + STATS
    for n in range(out_ref.shape[0]):
        out_ref[n, :rows, :] = mine_ref[:rows, :]
        out_ref[n, rows:, :] = other_ref[:rows, :]
    keys_ref[:HALF, :] = mine_ref[rows:, :]
    keys_ref[HALF:, :] = other_ref[rows:, :]


def spread_call(n, *args):
    return pl.pallas_call(
        spread_kernel,
        in_specs=[pl.BlockSpec(memory_space=pltpu.VMEM)] * 2,
        out_specs=[pl.BlockSpec(memory_space=pltpu.VMEM)] * 2,
        out_shape=[
            jax.ShapeDtypeStruct((n, 2 * (HALF + STATS), 2 * HEAD), BF16),
            jax.ShapeDtypeStruct((ROWS, 2 * HEAD), BF16),
        ],
        name="spread",
    )(*args)


def tile_kernel(count, first, waits, chips, *refs):
    refs = list(refs)
    qg_ref = refs.pop(0)
    blocks = [refs.pop(0) for _ in range(count)]
    if not first:
        old_ref = refs.pop(0)
    if waits:
        refs.pop(0)
    dq_ref = refs.pop(0)
    sums = [refs.pop(0) for _ in range(count)]
    acc_k, acc_v, kt_ref = refs
    step = pl.program_id(0)

    @pl.when(step == 0)
    def _():
        acc_k[...] = jnp.zeros_like(acc_k)
        acc_v[...] = jnp.zeros_like(acc_v)
        for n, kv_ref in enumerate(blocks):
            kt_ref[n] = kv_ref[:, :HEAD].astype(F32).T.astype(BF16)

    for chip in range(chips):
        qs, gs, lses, deltas = [], [], [], []
        for base in (0, HALF + STATS):
            qs.append(qg_ref[chip, base : base + HALF, :HEAD])
            gs.append(qg_ref[chip, base : base + HALF, HEAD:])
            stats = qg_ref[chip, base + HALF : base + HALF + STATS, :].astype(F32)
            stats = stats[0:1] + stats[1:2] + stats[2:3]
            lses.append(stats[:, :HALF])
            deltas.append(stats[:, HALF:])
        q = jnp.concatenate(qs, axis=0)
        g = jnp.concatenate(gs, axis=0)
        lse = jnp.concatenate(lses, axis=1)
        delta = jnp.concatenate(deltas, axis=1)
        total = None if first else old_ref[chip]
        for n, kv_ref in enumerate(blocks):
            s = lax.dot_general(kv_ref[:, :HEAD], q, NT, preferred_element_type=F32)
            p = jnp.exp2(s * (SCALE * LOG2E) - lse)
            dp = lax.dot_general(kv_ref[:, HEAD:], g, NT, preferred_element_type=F32)
            ds = (SCALE * p * (dp - delta)).astype(BF16)
            acc_v[n] += jnp.dot(p.astype(BF16), g, preferred_element_type=F32)
            acc_k[n] += jnp.dot(ds, q, preferred_element_type=F32)
            dq = jnp.dot(kt_ref[n], ds, preferred_element_type=F32)
            total = dq if total is None else total + dq
        dq_ref[chip] = total.astype(dq_ref.dtype)

    @pl.when(step == pl.num_programs(0) - 1)
    def _():
        for n, d_ref in enumerate(sums):
            d_ref[:, :HEAD] = acc_k[n]
            d_ref[:, HEAD:] = acc_v[n]


def tile_call(qg, blocks, old=None, after=None, last=False):
    first = old is None
    groups, rows, width = qg.shape
    count, keys = len(blocks), blocks[0].shape[0]
    chips = 4
    q_spec = pl.BlockSpec((chips, rows, width), lambda i: (i, 0, 0))
    kv_spec = pl.BlockSpec((keys, width), lambda i: (0, 0))
    dq_spec = pl.BlockSpec((chips, HEAD, ROWS), lambda i: (i, 0, 0))
    dq_shape = jax.ShapeDtypeStruct((groups, HEAD, ROWS), BF16 if last else F32)
    args, specs = [qg, *blocks], [q_spec] + [kv_spec] * count
    if not first:
        args.append(old)
        specs.append(dq_spec)
    if after is not None:
        args.append(after)
        specs.append(pl.BlockSpec(memory_space=pl.ANY))
    pairs = groups * ROWS * count * keys
    return pl.pallas_call(
        functools.partial(tile_kernel, count, first, after is not None, chips),
        grid=(groups // chips,),
        in_specs=specs,
        out_specs=[dq_spec] + [kv_spec] * count,
        out_shape=[dq_shape] + [jax.ShapeDtypeStruct((keys, width), F32)] * count,
        scratch_shapes=[
            pltpu.VMEM((count, keys, HEAD), F32),
            pltpu.VMEM((count, keys, HEAD), F32),
            pltpu.VMEM((count, HEAD, keys), BF16),
        ],
        compiler_params=pltpu.CompilerParams(vmem_limit_bytes=40 * 2**20),
        cost_estimate=pl.CostEstimate(
            flops=pairs * HEAD * 20, bytes_accessed=8 * 2**20, transcendentals=pairs
        ),
        name="tile",
    )(*args)


def shift(x, axis, by):
    n = lax.axis_size(axis)
    return lax.ppermute(x, axis, [(i, (i + by) % n) for i in range(n)])


def local(queries, key_rows, value_rows, attn_output, grad_output, row_lse):
    core = lax.axis_index("core")
    even = core == 0
    mine, send = pack_call(
        core, queries, key_rows, value_rows, attn_output, grad_output, row_lse
    )
    other = shift(send, "core", 1)
    peers = math.prod(lax.axis_size(a) for a in GROUP)
    spread, key_pack = spread_call(peers, mine, other)
    key_pair = jnp.concatenate([key_pack, shift(key_pack, "xh", 1)], axis=0)
    gathered = lax.all_to_all(spread, GROUP, 0, 0, tiled=True)
    keys = {0: key_pair}
    for by in (1, 2, 3):
        keys[by] = shift(keys[by - 1], "z", 1)
        keys[-by] = shift(keys[1 - by], "z", -1)
    keys[4] = jnp.concatenate(
        [shift(keys[3][:ROWS], "z", 1), shift(keys[-3][ROWS:], "z", -1)], axis=0
    )

    def low(x):
        return x.astype(BF16)

    total_q, own = tile_call(gathered, [keys[0]])
    total_q, du, dd = tile_call(gathered, [keys[-3], keys[3]], total_q)
    up, down = low(du), low(dd)
    up_in, down_in = shift(up, "z", 1), shift(down, "z", -1)
    total_q, far = tile_call(gathered, [keys[4]], total_q, up)
    far = low(far)
    after = far
    for by in (2, 1):
        total_q, du, dd = tile_call(
            gathered, [keys[-by], keys[by]], total_q, after, by == 1
        )
        up, down = low(du + up_in.astype(F32)), low(dd + down_in.astype(F32))
        up_in, down_in = shift(up, "z", 1), shift(down, "z", -1)
        after = up
    far_in = shift(far, "z", 4)
    returned = lax.all_to_all(total_q, GROUP, 0, 0, tiled=True)
    grad_pair = own + far_in.astype(F32) + up_in.astype(F32) + down_in.astype(F32)
    grad_kv = grad_pair[:ROWS] + shift(low(grad_pair[ROWS:]), "xh", 1).astype(F32)

    grad_q = jnp.sum(returned.astype(F32), axis=0).T
    grads = jnp.stack([grad_q, grad_kv[:, :HEAD], grad_kv[:, HEAD:]]).astype(BF16)
    kept = grads[:, :HALF]
    moved = shift(grads[:, HALF:], "core", 1)
    out = jnp.concatenate(
        [jnp.where(even, kept, moved), jnp.where(even, moved, kept)], axis=2
    )
    return out[0], out[1], out[2]


def solution(mesh):
    devices = mesh.devices.reshape(4, 2, 8, 2, 2)
    torus = Mesh(devices, AXES)
    rows = P(AXES, None)
    return jax.shard_map(
        local,
        mesh=torus,
        in_specs=(rows, rows, rows, rows, rows, P(None, AXES)),
        out_specs=(rows, rows, rows),
        check_vma=False,
    )
```

```python
import functools
import math

import jax
import jax.numpy as jnp
from jax import lax
from jax.experimental import pallas as pl
from jax.experimental.pallas import tpu as pltpu
from jax.sharding import Mesh, PartitionSpec as P

HEAD = 128
SCALE = HEAD**-0.5
LOG2E = math.log2(math.e)
AXES = ("y", "xh", "z", "xl", "core")
GROUP = ("y", "xl")
ROWS = 256
STATS = 16
HALF = 128
NT = (((1,), (1,)), ((), ()))
F32, BF16 = jnp.float32, jnp.bfloat16


def split3(x):
    hi = x.astype(BF16)
    rest = x - hi.astype(F32)
    mid = rest.astype(BF16)
    low = (rest - mid.astype(F32)).astype(BF16)
    return jnp.concatenate([hi.astype(F32), mid.astype(F32), low.astype(F32)], axis=0)


def pack_kernel(core_ref, q_ref, k_ref, v_ref, o_ref, g_ref, lse_ref, mine_ref, send_ref):
    def fill(head, qg, kv):
        cols = slice(head * HEAD, (head + 1) * HEAD)
        g = g_ref[:, cols]
        products = g.astype(F32) * o_ref[:, cols].astype(F32)
        delta = jnp.sum(products.T, axis=0, keepdims=True)
        lse = lse_ref[head : head + 1, :] * LOG2E
        terms = jnp.concatenate([split3(lse), split3(delta)], axis=1)
        terms = jnp.concatenate([terms, jnp.zeros((STATS - 3, 2 * HALF), F32)], axis=0)
        qg[:HALF, :HEAD] = q_ref[:, cols]
        qg[:HALF, HEAD:] = g
        qg[HALF:, :] = terms.astype(BF16)
        kv[:, :HEAD] = k_ref[:, cols]
        kv[:, HEAD:] = v_ref[:, cols]

    def halves(ref):
        return ref.at[: HALF + STATS], ref.at[HALF + STATS :]

    for core in range(2):

        @pl.when(core_ref[0] == core)
        def _():
            fill(core, *halves(mine_ref))
            fill(1 - core, *halves(send_ref))


def pack_call(core, *args):
    width = 2 * HEAD
    return pl.pallas_call(
        pack_kernel,
        in_specs=[pl.BlockSpec(memory_space=pltpu.SMEM)]
        + [pl.BlockSpec(memory_space=pltpu.VMEM)] * 6,
        out_specs=[pl.BlockSpec(memory_space=pltpu.VMEM)] * 2,
        out_shape=[jax.ShapeDtypeStruct((2 * HALF + STATS, width), BF16)] * 2,
        name="pack",
    )(core.reshape(1), *args)


def spread_kernel(mine_ref, other_ref, _, out_ref):
    rows = HALF + STATS
    for n in range(out_ref.shape[0]):
        out_ref[n, :rows, :] = mine_ref[:rows, :]
        out_ref[n, rows:, :] = other_ref[:rows, :]


def spread_call(n, *args):
    return pl.pallas_call(
        spread_kernel,
        in_specs=[pl.BlockSpec(memory_space=pltpu.VMEM)] * 3,
        out_specs=pl.BlockSpec(memory_space=pltpu.VMEM),
        out_shape=jax.ShapeDtypeStruct((n, 2 * (HALF + STATS), 2 * HEAD), BF16),
        name="spread",
    )(*args)


def tile_kernel(count, first, waits, chips, *refs):
    refs = list(refs)
    qg_ref = refs.pop(0)
    blocks = [refs.pop(0) for _ in range(count)]
    if not first:
        old_ref = refs.pop(0)
    if waits:
        refs.pop(0)
    dq_ref = refs.pop(0)
    sums = [refs.pop(0) for _ in range(count)]
    acc_k, acc_v, kt_ref = refs
    step = pl.program_id(0)

    @pl.when(step == 0)
    def _():
        acc_k[...] = jnp.zeros_like(acc_k)
        acc_v[...] = jnp.zeros_like(acc_v)
        for n, kv_ref in enumerate(blocks):
            kt_ref[n] = kv_ref[:, :HEAD].astype(F32).T.astype(BF16)

    for chip in range(chips):
        qs, gs, lses, deltas = [], [], [], []
        for base in (0, HALF + STATS):
            qs.append(qg_ref[chip, base : base + HALF, :HEAD])
            gs.append(qg_ref[chip, base : base + HALF, HEAD:])
            stats = qg_ref[chip, base + HALF : base + HALF + STATS, :].astype(F32)
            stats = stats[0:1] + stats[1:2] + stats[2:3]
            lses.append(stats[:, :HALF])
            deltas.append(stats[:, HALF:])
        q = jnp.concatenate(qs, axis=0)
        g = jnp.concatenate(gs, axis=0)
        lse = jnp.concatenate(lses, axis=1)
        delta = jnp.concatenate(deltas, axis=1)
        total = None if first else old_ref[chip]
        for n, kv_ref in enumerate(blocks):
            s = lax.dot_general(kv_ref[:, :HEAD], q, NT, preferred_element_type=F32)
            p = jnp.exp2(s * (SCALE * LOG2E) - lse)
            dp = lax.dot_general(kv_ref[:, HEAD:], g, NT, preferred_element_type=F32)
            ds = (SCALE * p * (dp - delta)).astype(BF16)
            acc_v[n] += jnp.dot(p.astype(BF16), g, preferred_element_type=F32)
            acc_k[n] += jnp.dot(ds, q, preferred_element_type=F32)
            dq = jnp.dot(kt_ref[n], ds, preferred_element_type=F32)
            total = dq if total is None else total + dq
        dq_ref[chip] = total.astype(dq_ref.dtype)

    @pl.when(step == pl.num_programs(0) - 1)
    def _():
        for n, d_ref in enumerate(sums):
            d_ref[:, :HEAD] = acc_k[n]
            d_ref[:, HEAD:] = acc_v[n]


def tile_call(qg, blocks, old=None, after=None, last=False):
    first = old is None
    groups, rows, width = qg.shape
    count, keys = len(blocks), blocks[0].shape[0]
    chips = 4
    q_spec = pl.BlockSpec((chips, rows, width), lambda i: (i, 0, 0))
    kv_spec = pl.BlockSpec((keys, width), lambda i: (0, 0))
    dq_spec = pl.BlockSpec((chips, HEAD, ROWS), lambda i: (i, 0, 0))
    dq_shape = jax.ShapeDtypeStruct((groups, HEAD, ROWS), BF16 if last else F32)
    args, specs = [qg, *blocks], [q_spec] + [kv_spec] * count
    if not first:
        args.append(old)
        specs.append(dq_spec)
    if after is not None:
        args.append(after)
        specs.append(pl.BlockSpec(memory_space=pl.ANY))
    pairs = groups * ROWS * count * keys
    return pl.pallas_call(
        functools.partial(tile_kernel, count, first, after is not None, chips),
        grid=(groups // chips,),
        in_specs=specs,
        out_specs=[dq_spec] + [kv_spec] * count,
        out_shape=[dq_shape] + [jax.ShapeDtypeStruct((keys, width), F32)] * count,
        scratch_shapes=[
            pltpu.VMEM((count, keys, HEAD), F32),
            pltpu.VMEM((count, keys, HEAD), F32),
            pltpu.VMEM((count, HEAD, keys), BF16),
        ],
        compiler_params=pltpu.CompilerParams(vmem_limit_bytes=40 * 2**20),
        cost_estimate=pl.CostEstimate(
            flops=pairs * HEAD * 20, bytes_accessed=8 * 2**20, transcendentals=pairs
        ),
        name="tile",
    )(*args)


def shift(x, axis, by):
    n = lax.axis_size(axis)
    return lax.ppermute(x, axis, [(i, (i + by) % n) for i in range(n)])


def local(queries, key_rows, value_rows, attn_output, grad_output, row_lse):
    core = lax.axis_index("core")
    even = core == 0
    mine, send = pack_call(
        core, queries, key_rows, value_rows, attn_output, grad_output, row_lse
    )
    other = shift(send, "core", 1)
    peers = math.prod(lax.axis_size(a) for a in GROUP)
    key_pack = jnp.concatenate([mine[HALF + STATS :], other[HALF + STATS :]], axis=0)
    partner = shift(key_pack, "xh", 1)
    key_pair = jnp.concatenate([key_pack, partner], axis=0)
    spread = spread_call(peers, mine, other, partner)
    gathered = lax.all_to_all(spread, GROUP, 0, 0, tiled=True)
    keys = {0: key_pair}
    for by in (1, 2, 3):
        keys[by] = shift(keys[by - 1], "z", 1)
        keys[-by] = shift(keys[1 - by], "z", -1)
    total_q, own = tile_call(gathered, [keys[0]])
    zero = jnp.minimum(jnp.abs(own[0, 0]), 0.0).astype(BF16)
    keys[4] = jnp.concatenate(
        [shift(keys[3][:ROWS] + zero, "z", 1), shift(keys[-3][ROWS:] + zero, "z", -1)],
        axis=0,
    )

    def low(x):
        return x.astype(BF16)

    total_q, du, dd = tile_call(gathered, [keys[-3], keys[3]], total_q)
    up, down = low(du), low(dd)
    up_in, down_in = shift(up, "z", 1), shift(down, "z", -1)
    total_q, far = tile_call(gathered, [keys[4]], total_q, up)
    far = low(far)
    after = far
    for by in (2, 1):
        total_q, du, dd = tile_call(
            gathered, [keys[-by], keys[by]], total_q, after, by == 1
        )
        up, down = low(du + up_in.astype(F32)), low(dd + down_in.astype(F32))
        up_in, down_in = shift(up, "z", 1), shift(down, "z", -1)
        after = up
    far_in = shift(far, "z", 4)
    returned = lax.all_to_all(total_q, GROUP, 0, 0, tiled=True)
    grad_pair = own + far_in.astype(F32) + up_in.astype(F32) + down_in.astype(F32)
    grad_kv = grad_pair[:ROWS] + shift(low(grad_pair[ROWS:]), "xh", 1).astype(F32)

    grad_q = jnp.sum(returned.astype(F32), axis=0).T
    grads = jnp.stack([grad_q, grad_kv[:, :HEAD], grad_kv[:, HEAD:]]).astype(BF16)
    kept = grads[:, :HALF]
    moved = shift(grads[:, HALF:], "core", 1)
    out = jnp.concatenate(
        [jnp.where(even, kept, moved), jnp.where(even, moved, kept)], axis=2
    )
    return out[0], out[1], out[2]


def solution(mesh):
    devices = mesh.devices.reshape(4, 2, 8, 2, 2)
    torus = Mesh(devices, AXES)
    rows = P(AXES, None)
    return jax.shard_map(
        local,
        mesh=torus,
        in_specs=(rows, rows, rows, rows, rows, P(None, AXES)),
        out_specs=(rows, rows, rows),
        check_vma=False,
    )
```

```python
import functools
import math

import jax
import jax.numpy as jnp
from jax import lax
from jax.experimental import pallas as pl
from jax.experimental.pallas import tpu as pltpu
from jax.sharding import Mesh, PartitionSpec as P

HEAD = 128
SCALE = HEAD**-0.5
LOG2E = math.log2(math.e)
AXES = ("y", "xh", "z", "xl", "core")
GROUP = ("y", "xl")
ROWS = 256
STATS = 16
HALF = 128
NT = (((1,), (1,)), ((), ()))
F32, BF16 = jnp.float32, jnp.bfloat16


def split3(x):
    hi = x.astype(BF16)
    rest = x - hi.astype(F32)
    mid = rest.astype(BF16)
    low = (rest - mid.astype(F32)).astype(BF16)
    return jnp.concatenate([hi.astype(F32), mid.astype(F32), low.astype(F32)], axis=0)


def pack_kernel(core_ref, q_ref, k_ref, v_ref, o_ref, g_ref, lse_ref, qg_ref, kv_ref, send_ref):
    def fill(head, qg, kv):
        cols = slice(head * HEAD, (head + 1) * HEAD)
        g = g_ref[:, cols]
        products = g.astype(F32) * o_ref[:, cols].astype(F32)
        delta = jnp.sum(products.T, axis=0, keepdims=True)
        lse = lse_ref[head : head + 1, :] * LOG2E
        terms = jnp.concatenate([split3(lse), split3(delta)], axis=1)
        terms = jnp.concatenate([terms, jnp.zeros((STATS - 3, 2 * HALF), F32)], axis=0)
        qg[:HALF, :HEAD] = q_ref[:, cols]
        qg[:HALF, HEAD:] = g
        qg[HALF:, :] = terms.astype(BF16)
        kv[:, :HEAD] = k_ref[:, cols]
        kv[:, HEAD:] = v_ref[:, cols]

    send_qg = send_ref.at[: HALF + STATS]
    send_kv = send_ref.at[HALF + STATS :]
    for core in range(2):

        @pl.when(core_ref[0] == core)
        def _():
            fill(core, qg_ref, kv_ref)
            fill(1 - core, send_qg, send_kv)


def pack_call(core, *args):
    width = 2 * HEAD
    return pl.pallas_call(
        pack_kernel,
        in_specs=[pl.BlockSpec(memory_space=pltpu.SMEM)]
        + [pl.BlockSpec(memory_space=pltpu.VMEM)] * 6,
        out_specs=[pl.BlockSpec(memory_space=pltpu.VMEM)] * 3,
        out_shape=[
            jax.ShapeDtypeStruct((HALF + STATS, width), BF16),
            jax.ShapeDtypeStruct((HALF, width), BF16),
            jax.ShapeDtypeStruct((2 * HALF + STATS, width), BF16),
        ],
        name="pack",
    )(core.reshape(1), *args)


def spread_kernel(mine_ref, kv_ref, other_ref, out_ref, keys_ref):
    rows = HALF + STATS
    for n in range(out_ref.shape[0]):
        out_ref[n, :rows, :] = mine_ref[...]
        out_ref[n, rows:, :] = other_ref[:rows, :]
    keys_ref[:HALF, :] = kv_ref[...]
    keys_ref[HALF:, :] = other_ref[rows:, :]


def spread_call(n, *args):
    return pl.pallas_call(
        spread_kernel,
        in_specs=[pl.BlockSpec(memory_space=pltpu.VMEM)] * 3,
        out_specs=[pl.BlockSpec(memory_space=pltpu.VMEM)] * 2,
        out_shape=[
            jax.ShapeDtypeStruct((n, 2 * (HALF + STATS), 2 * HEAD), BF16),
            jax.ShapeDtypeStruct((ROWS, 2 * HEAD), BF16),
        ],
        name="spread",
    )(*args)


def tile_kernel(first, chips, *refs):
    if first:
        qg_ref, kv1_ref, kv2_ref, dq_ref, d1_ref, d2_ref, acc_k, acc_v, kt_ref = refs
    else:
        qg_ref, kv1_ref, kv2_ref, old_ref, _, dq_ref, d1_ref, d2_ref, acc_k, acc_v, kt_ref = refs
    step = pl.program_id(0)
    blocks = (kv1_ref, kv2_ref)

    @pl.when(step == 0)
    def _():
        acc_k[...] = jnp.zeros_like(acc_k)
        acc_v[...] = jnp.zeros_like(acc_v)
        for n, kv_ref in enumerate(blocks):
            kt_ref[n] = kv_ref[:, :HEAD].astype(F32).T.astype(BF16)

    for chip in range(chips):
        qs, gs, lses, deltas = [], [], [], []
        for base in (0, HALF + STATS):
            qs.append(qg_ref[chip, base : base + HALF, :HEAD])
            gs.append(qg_ref[chip, base : base + HALF, HEAD:])
            stats = qg_ref[chip, base + HALF : base + HALF + STATS, :].astype(F32)
            stats = stats[0:1] + stats[1:2] + stats[2:3]
            lses.append(stats[:, :HALF])
            deltas.append(stats[:, HALF:])
        q = jnp.concatenate(qs, axis=0)
        g = jnp.concatenate(gs, axis=0)
        lse = jnp.concatenate(lses, axis=1)
        delta = jnp.concatenate(deltas, axis=1)
        total = None if first else old_ref[chip]
        for n, kv_ref in enumerate(blocks):
            s = lax.dot_general(kv_ref[:, :HEAD], q, NT, preferred_element_type=F32)
            p = jnp.exp2(s * (SCALE * LOG2E) - lse)
            dp = lax.dot_general(kv_ref[:, HEAD:], g, NT, preferred_element_type=F32)
            ds = (SCALE * p * (dp - delta)).astype(BF16)
            acc_v[n] += jnp.dot(p.astype(BF16), g, preferred_element_type=F32)
            acc_k[n] += jnp.dot(ds, q, preferred_element_type=F32)
            dq = jnp.dot(kt_ref[n], ds, preferred_element_type=F32)
            total = dq if total is None else total + dq
        dq_ref[chip] = total.astype(dq_ref.dtype)

    @pl.when(step == pl.num_programs(0) - 1)
    def _():
        for n, d_ref in enumerate((d1_ref, d2_ref)):
            d_ref[:, :HEAD] = acc_k[n]
            d_ref[:, HEAD:] = acc_v[n]


def tile_call(qg, kv1, kv2, old, after, last):
    first = old is None
    groups, rows, width = qg.shape
    chips = 2
    q_spec = pl.BlockSpec((chips, rows, width), lambda i: (i, 0, 0))
    keys = kv1.shape[0]
    kv_spec = pl.BlockSpec((keys, width), lambda i: (0, 0))
    dq_spec = pl.BlockSpec((chips, HEAD, ROWS), lambda i: (i, 0, 0))
    pairs = groups * ROWS * 2 * keys
    return pl.pallas_call(
        functools.partial(tile_kernel, first, chips),
        grid=(groups // chips,),
        in_specs=[q_spec, kv_spec, kv_spec]
        + ([] if first else [dq_spec, pl.BlockSpec(memory_space=pl.ANY)]),
        out_specs=[dq_spec, kv_spec, kv_spec],
        out_shape=[
            jax.ShapeDtypeStruct((groups, HEAD, ROWS), BF16 if last else F32),
            jax.ShapeDtypeStruct((keys, width), F32),
            jax.ShapeDtypeStruct((keys, width), F32),
        ],
        scratch_shapes=[
            pltpu.VMEM((2, keys, HEAD), F32),
            pltpu.VMEM((2, keys, HEAD), F32),
            pltpu.VMEM((2, HEAD, keys), BF16),
        ],
        compiler_params=pltpu.CompilerParams(vmem_limit_bytes=40 * 2**20),
        cost_estimate=pl.CostEstimate(
            flops=pairs * HEAD * 20, bytes_accessed=8 * 2**20, transcendentals=pairs
        ),
        name="tile",
    )(*((qg, kv1, kv2) if first else (qg, kv1, kv2, old, after)))


def shift(x, axis, by):
    n = lax.axis_size(axis)
    return lax.ppermute(x, axis, [(i, (i + by) % n) for i in range(n)])


def local(queries, key_rows, value_rows, attn_output, grad_output, row_lse):
    core = lax.axis_index("core")
    even = core == 0
    mine_q, mine_kv, send = pack_call(
        core, queries, key_rows, value_rows, attn_output, grad_output, row_lse
    )
    other = shift(send, "core", 1)
    peers = math.prod(lax.axis_size(a) for a in GROUP)
    spread, key_pack = spread_call(peers, mine_q, mine_kv, other)
    key_pair = jnp.concatenate([key_pack, shift(key_pack, "xh", 1)], axis=0)
    gathered = lax.all_to_all(spread, GROUP, 0, 0, tiled=True)
    keys = {0: key_pair}
    for by in (1, 2, 3):
        keys[by] = shift(keys[by - 1], "z", 1)
        keys[-by] = shift(keys[1 - by], "z", -1)
    keys[4] = jnp.concatenate(
        [shift(keys[3][:ROWS], "z", 1), shift(keys[-3][ROWS:], "z", -1)], axis=0
    )

    def low(x):
        return x.astype(BF16)

    total_q, du, dd = tile_call(gathered, keys[-3], keys[3], None, None, False)
    up, down = low(du), low(dd)
    up_in, down_in = shift(up, "z", 1), shift(down, "z", -1)
    total_q, far, own = tile_call(gathered, keys[4], keys[0], total_q, up, False)
    far = low(far)
    after = far
    for by in (2, 1):
        total_q, du, dd = tile_call(gathered, keys[-by], keys[by], total_q, after, by == 1)
        up, down = low(du + up_in.astype(F32)), low(dd + down_in.astype(F32))
        up_in, down_in = shift(up, "z", 1), shift(down, "z", -1)
        after = up
    far_in = shift(far, "z", 4)
    returned = lax.all_to_all(total_q, GROUP, 0, 0, tiled=True)
    grad_pair = own + far_in.astype(F32) + up_in.astype(F32) + down_in.astype(F32)
    grad_kv = grad_pair[:ROWS] + shift(low(grad_pair[ROWS:]), "xh", 1).astype(F32)

    grad_q = jnp.sum(returned.astype(F32), axis=0).T
    grads = jnp.stack([grad_q, grad_kv[:, :HEAD], grad_kv[:, HEAD:]]).astype(BF16)
    kept = grads[:, :HALF]
    moved = shift(grads[:, HALF:], "core", 1)
    out = jnp.concatenate(
        [jnp.where(even, kept, moved), jnp.where(even, moved, kept)], axis=2
    )
    return out[0], out[1], out[2]


def solution(mesh):
    devices = mesh.devices.reshape(4, 2, 8, 2, 2)
    torus = Mesh(devices, AXES)
    rows = P(AXES, None)
    return jax.shard_map(
        local,
        mesh=torus,
        in_specs=(rows, rows, rows, rows, rows, P(None, AXES)),
        out_specs=(rows, rows, rows),
        check_vma=False,
    )
```
